512 devices in a mesh: depth: 8 (over z), block: 64 (over x, y, core).
Axes of the slice: x: 4, y: 8, z: 8, core: 2. Of those that a mesh axis runs over, the one named last changes fastest.
Arguments:
- sensitivity: float32 [16384, 8, 1024], P(('depth', 'block')), as said below
- owners: int32 [16384, 8], P(('depth', 'block')), may hold values from 0 to 63, all different within a row; in each aligned block of 32 rows (0 to 31, 32 to 63, ...) at most 8 rows name the same one
- local_block: int32 [16384, 8], P(('depth', 'block')), may hold values from 0 to 3
- station_ids: int32 [16384], P(('depth', 'block')), may hold values from 0 to 1023
- kept: int32 [16384], P(('depth', 'block')), may hold values 0 or 1
- times: float32 [16384], P(('depth', 'block')), may hold values from -6 to 6
- hit_counts: int32 [8, 256, 128], P('depth', 'block'), may hold values from 0 to 63
Outputs:
- model_update: float32 [8, 256, 128], P('depth', 'block')
- station_update: float32 [1024], replicated
- ray_direction: float32 [16384], P(('depth', 'block'))
The draws below stay inside these ranges and needn't reach their ends.
Inputs may be any that keep to these rules, and one draw needn't show every extreme that they name: Within a row the 8 owners differ; in the rows of one device no owner is named more than 8 times, and in some device one owner exactly 8 times. `sensitivity`: every entry is at most 16 / sqrt(8192) in magnitude.
All inputs are finite; a program needn't handle non-finite values. No bound on the sum of `kept` on one device may be relied on, other than what follows from the above.
Results may differ from the reference program's by a relative error of at most 0.0003.
Values sent between devices are 32-bit elements; how exact they have to be, the bound alone decides.
A program may use at most 64 MiB of HBM per device.

```python
import math
import jax
import jax.numpy as jnp
import numpy as np
from jax import lax

RAY_DEV = 32
K = 8
BLK_DEV = 4
CELLS = 128
NSTA = 1024
ITERS = 2
CAP = 8
LAYERS = 8
NBLOCKS = 256
RAYS = 16384
N_BLOCK = 64


def draw_sensitivity(key, part):
    extent = (RAYS, K, LAYERS * CELLS)
    deviation = 4.0 / math.sqrt(K * LAYERS * CELLS)
    samples = jnp.clip(jax.random.normal(key, extent, jnp.float32), -4.0, 4.0)
    return (samples * deviation).astype(jnp.float32)


def place_ends(entries, key, low, top_value):
    index_at = [jax.random.randint(jax.random.fold_in(key, axis), (), 0, length) for axis, length in enumerate(entries.shape)]
    longest = entries.shape.index(max(entries.shape))
    next_to = index_at[:longest] + [(index_at[longest] + 1) % entries.shape[longest]] + index_at[longest + 1:]
    return entries.at[tuple(index_at)].set(low).at[tuple(next_to)].set(top_value)


def block_scale(key, dims, cuts, low, largest):
    factor_of = 1.0
    for dim, parts in cuts:
        heights = jax.random.uniform(jax.random.fold_in(jax.random.fold_in(key, 6), dim), (parts,), jnp.float32, low / len(cuts), largest / len(cuts))
        factor_of = factor_of * jnp.repeat(jnp.exp(heights), dims[dim] // parts).reshape((-1,) + (1,) * (len(dims) - 1 - dim))
    return factor_of


def cumulative_ranks(number_of, slope):
    weights = [(1 << 20) // math.isqrt(grade ** slope) + 1 for grade in range(1, number_of + 1)]
    scale = 1 + sum(weights) // (1 << 30)
    return np.cumsum(np.array([max(1, weight // scale) for weight in weights]))


def ranked(rng, dims, amount, skew):
    grid = cumulative_ranks(amount, skew)
    pick = jax.random.randint(jax.random.fold_in(rng, 1), dims, 0, int(grid[amount - 1]))
    rank = jnp.searchsorted(jnp.asarray(grid, jnp.int32), pick, side="right")
    return jax.random.permutation(jax.random.fold_in(rng, 2), amount)[rank].astype(jnp.int32)


def assign_block(rng, own, number, rows, amount, top, most, skew):
    sequence = jax.random.permutation(rng, amount)
    heavy_load, ordinary = portions_of(amount, rows * top, most, skew, True), portions_of(amount, rows * top, most, skew, False)
    places = jnp.arange(amount)

    def named(sizes, offset_by):
        used = int((sizes > 0).sum())
        fixed = max(1, used // 4)
        passed = fixed + (places - fixed + offset_by * (used - fixed)) % max(1, amount - fixed)
        return jnp.zeros((amount,), jnp.int32).at[sequence[jnp.where(places < fixed, places, passed)]].set(jnp.asarray(sizes, jnp.int32))

    sizes = jnp.where(number % 4 == 0, named(heavy_load, number // 4), named(ordinary, number - number // 4 - 1))
    mixed = jax.random.permutation(jax.random.fold_in(own, 3), amount)
    source_of, sink = mixed[0:amount // 2 * 2:2], mixed[1:amount // 2 * 2:2]
    slack = jnp.minimum(sizes[source_of] - 1, most - sizes[sink]) // 2
    slack = jnp.where((source_of == sequence[0]) | (sink == sequence[0]) | (sizes[sink] == 0), 0, jnp.maximum(slack, 0))
    passed = jax.random.randint(jax.random.fold_in(own, 4), (amount // 2,), 0, 1 << 20) % (slack + 1)
    sizes = sizes.at[source_of].add(-passed).at[sink].add(passed)
    labels = jnp.searchsorted(jnp.cumsum(sizes), jnp.arange(rows * top), side="right").astype(jnp.int32)
    grid = labels.reshape(top, rows).T
    grid = grid[jax.random.permutation(jax.random.fold_in(own, 1), rows)]
    offset_by = jax.random.randint(jax.random.fold_in(own, 2), (rows, 1), 0, top)
    return jnp.take_along_axis(grid, (jnp.arange(top)[None, :] + offset_by) % top, axis=1)


def portions_of(number_of, total, limit, skew, full):
    loads = [(1 << 20) // math.isqrt(grade ** skew) + 1 for grade in range(1, number_of + 1)]
    largest = limit if full else min(limit, max(-(-total // number_of), total * loads[0] // sum(loads)))
    least = 1 if total - largest >= number_of - 1 else 0
    counts, spare = [largest] + [least] * (number_of - 1), total - largest - least * (number_of - 1)
    while spare > 0:
        candidates = [i for i in range(1, number_of) if counts[i] < largest] or [i for i in range(1, number_of) if counts[i] < limit]
        mass, left = sum([loads[i] for i in candidates]), spare
        for i in candidates:
            addition = min(limit - counts[i], max(1, left * loads[i] // mass), spare)
            counts[i] = counts[i] + addition
            spare = spare - addition
    return np.array(counts)


def scatter_about(own_key, shape, spread, reach, cuts=(), dtype=jnp.bfloat16):
    array = jax.random.normal(own_key, shape, jnp.float32) * spread
    if len(cuts) > 0:
        array = block_scale(own_key, shape, cuts, -0.22, 0.18) * array
    return jnp.clip(array, min=-reach, max=reach).astype(dtype)


def setup_inputs(seed: int = 0) -> dict:
    key_list = jax.random.split(jax.random.key(seed), 8)
    sensitivity = draw_sensitivity(jax.random.fold_in(key_list[7], 71), 0)
    owners_keys = jax.random.split(jax.random.fold_in(key_list[1], 1), RAYS // RAY_DEV)
    owners_turns = jax.random.permutation(jax.random.fold_in(key_list[1], 3), RAYS // RAY_DEV)
    owners = jax.vmap(lambda own, number: assign_block(jax.random.fold_in(key_list[1], 2), own, number, RAY_DEV, N_BLOCK, K, CAP, 2))(owners_keys, owners_turns).reshape((RAYS, K))
    local_block = place_ends(jax.random.randint(key_list[2], (RAYS, K), 0, BLK_DEV), jax.random.fold_in(key_list[2], 1), 0, BLK_DEV - 1).astype(jnp.int32)
    station_ids = place_ends(ranked(key_list[3], (RAYS,), NSTA, 2), jax.random.fold_in(key_list[3], 3), 0, NSTA - 1).astype(jnp.int32)
    kept = place_ends((jax.random.randint(key_list[4], (RAYS,), 0, 4) < 3).astype(jnp.int32), jax.random.fold_in(key_list[4], 1), 0, 1)
    times = scatter_about(key_list[5], (RAYS,), 1.0, 6.0, ((0, 512),), jnp.float32)
    hit_counts = place_ends(jax.random.randint(key_list[6], (LAYERS, NBLOCKS, CELLS), 0, 64), jax.random.fold_in(key_list[6], 1), 0, 63).astype(jnp.int32)
    return dict(sensitivity=sensitivity, owners=owners, local_block=local_block, station_ids=station_ids, kept=kept, times=times, hit_counts=hit_counts)


epsilon = 1e-06

def reference(sensitivity, owners, local_block, station_ids, kept, times, hit_counts):
    width = LAYERS * CELLS
    column_scale = 1.0 / jnp.sqrt(1.0 + hit_counts.astype(jnp.float32))
    kept_rows = kept.astype(jnp.float32)
    global_block = (owners * BLK_DEV + local_block).astype(jnp.int32)
    groups = RAYS // RAY_DEV
    sens_groups = sensitivity.reshape(groups, RAY_DEV, K, width)
    block_groups = global_block.reshape(groups, RAY_DEV, K)

    def forward(model, stations):
        rows_all = (model * column_scale).transpose(1, 0, 2).reshape(NBLOCKS, width)

        def one_group(item):
            pieces, blocks = item
            return lax.optimization_barrier(jnp.sum(pieces * rows_all[blocks], axis=(1, 2)))
        kernel = lax.map(one_group, (sens_groups, block_groups)).reshape(RAYS)
        return kept_rows * (kernel + stations[station_ids])

    def adjoint(unit):
        unit_groups = unit.reshape(groups, RAY_DEV)

        def add_group(total, item):
            pieces, blocks, weights = item
            contrib = (pieces * weights[:, None, None]).reshape(RAY_DEV * K, width)
            return (total + jax.ops.segment_sum(contrib, blocks.reshape(-1), num_segments=NBLOCKS), None)
        total, unused = lax.scan(add_group, jnp.zeros((NBLOCKS, width), jnp.float32), (sens_groups, block_groups, unit_groups))
        model = total.reshape(NBLOCKS, LAYERS, CELLS).transpose(1, 0, 2) * column_scale
        stations = jax.ops.segment_sum(unit, station_ids, num_segments=NSTA)
        return (model, stations)
    raw = kept_rows * times
    beta_value = jnp.sqrt(jnp.sum(raw * raw) + epsilon)
    unit = raw / beta_value
    grad_model, grad_station = adjoint(unit)
    alpha_value = jnp.sqrt(jnp.sum(grad_model * grad_model) + jnp.sum(grad_station * grad_station) + epsilon)
    dir_model = grad_model / alpha_value
    dir_station = grad_station / alpha_value
    search_model, search_station = (dir_model, dir_station)
    sol_model = jnp.zeros_like(dir_model)
    sol_station = jnp.zeros_like(dir_station)
    phi_bar = beta_value
    rho_bar = alpha_value
    for iteration in range(ITERS):
        raw = forward(dir_model, dir_station) - alpha_value * unit
        beta_value = jnp.sqrt(jnp.sum(raw * raw) + epsilon)
        unit = raw / beta_value
        grad_model, grad_station = adjoint(unit)
        grad_model = grad_model - beta_value * dir_model
        grad_station = grad_station - beta_value * dir_station
        alpha_value = jnp.sqrt(jnp.sum(grad_model * grad_model) + jnp.sum(grad_station * grad_station) + epsilon)
        dir_model = grad_model / alpha_value
        dir_station = grad_station / alpha_value
        rho_value = jnp.sqrt(rho_bar * rho_bar + beta_value * beta_value)
        cosine = rho_bar / rho_value
        sine_value = beta_value / rho_value
        theta_value = sine_value * alpha_value
        rho_bar = -cosine * alpha_value
        phi_value = cosine * phi_bar
        phi_bar = sine_value * phi_bar
        sol_model = sol_model + phi_value / rho_value * search_model
        sol_station = sol_station + phi_value / rho_value * search_station
        search_model = dir_model - theta_value / rho_value * search_model
        search_station = dir_station - theta_value / rho_value * search_station
    return (column_scale * sol_model, sol_station, unit)
```

```python
import functools

import jax
import jax.numpy as jnp
from jax import lax
from jax.experimental import pallas as pl
from jax.experimental.pallas import tpu as pltpu
from jax.sharding import PartitionSpec as P

NX, NY, NZ = 4, 8, 8
EPS = 1e-06
F32 = jnp.float32
BF16 = jnp.bfloat16
HIGHEST = lax.Precision.HIGHEST
MESH = pl.DeviceIdType.MESH

META, ROWS, CSZ, CSY, CST, FX, FY, FZ = range(8)
S1X, S1Y, S1Z, S2Y, S2Z, S2X, S3Z, S3Y, A2Y, A2Z, A2X, A1X, A1Y, A1Z, EX = range(15)
STAGES = 8 + 2 * 15


def iota(shape, dim):
    return lax.broadcasted_iota(jnp.int32, shape, dim)


def total(tile):
    return jnp.sum(jnp.sum(tile, axis=0, keepdims=True), axis=1, keepdims=True)


def split(value):
    high = value.astype(BF16)
    return high, (value - high.astype(F32)).astype(BF16)


def dot(a, b):
    return jnp.dot(a, b, preferred_element_type=F32)


def dot_nt(a, b):
    return lax.dot_general(
        a, b, (((1,), (1,)), ((), ())), precision=HIGHEST, preferred_element_type=F32
    )


def kernel(
    sens, owners, local_block, station_ids, kept, times, hits,
    out_model, out_station, out_ray,
    rows, meta, ohr, ohc, cs_own, csz, csy, cst, fin, fx, fy, fz,
    sx, sy, sz, rx, ry, rz, s2y, s2z, s2x, r2y, r2z, r2x, s3z, s3y, r3z, r3y,
    a2y, a2z, a2x, g2y, g2z, g2x, a1x, gx, gy, gz, ex,
    local_sem, send_sem, recv_sem,
):
    z = lax.axis_index("depth")
    b = lax.axis_index("block")
    c = lax.rem(b, 2)
    y = lax.rem(lax.div(b, 2), NY)
    x = lax.div(b, 2 * NY)
    axes = {
        "x": (NX, x, lambda p: (z, (p * NY + y) * 2 + c)),
        "y": (NY, y, lambda p: (z, (x * NY + p) * 2 + c)),
        "z": (NZ, z, lambda p: (p, b)),
    }
    sibling = (z, (x * NY + y) * 2 + 1 - c)

    own_rows = pltpu.make_async_copy(
        sens.at[:, :, pl.ds(pl.multiple_of(c * 512, 512), 512)], rows.at[c], local_sem
    )
    own_rows.start()

    barrier = pltpu.get_barrier_semaphore()
    pl.semaphore_signal(barrier, inc=1, device_id=sibling, device_id_type=MESH)
    for name in "xyz":
        n, me, peer = axes[name]
        for step in range(1, n):
            pl.semaphore_signal(
                barrier, inc=1, device_id=peer(lax.rem(me + step, n)), device_id_type=MESH
            )

    blocks = (owners[...] * 4 + local_block[...]).astype(F32)
    eye8 = (iota((8, 8), 0) == iota((8, 8), 1)).astype(F32)
    spread = (lax.shift_right_logical(iota((32, 256), 1), 3) == iota((32, 256), 0)).astype(F32)
    by_slot = jnp.dot(
        dot_nt(eye8, blocks), spread, precision=HIGHEST, preferred_element_type=F32
    )
    slot_of = jnp.bitwise_and(iota((8, 256), 1), 7)
    block_row = jnp.sum(
        jnp.where(iota((8, 256), 0) == slot_of, by_slot, 0.0), axis=0, keepdims=True
    )
    keep = kept[...].astype(F32)
    ids = station_ids[...]
    scale = 1.0 / jnp.sqrt(1.0 + hits[0].astype(F32))
    meta[c] = jnp.zeros((2, 8, 128), F32)
    meta[c, 0, 0:1, :] = block_row[:, 0:128]
    meta[c, 0, 1:2, :] = block_row[:, 128:256]
    meta[c, 0, 2:3, 0:32] = keep * times[...]
    meta[c, 0, 3:4, 0:32] = keep
    meta[c, 0, 4:5, 0:32] = lax.shift_right_logical(ids, 7).astype(F32)
    meta[c, 0, 5:6, 0:32] = jnp.bitwise_and(ids, 127).astype(F32)
    meta[c, 1, 0:4, :] = jnp.where(c == 0, scale, 0.0)
    meta[c, 1, 4:8, :] = jnp.where(c == 1, scale, 0.0)

    pl.semaphore_wait(barrier, 1 + (NX - 1) + (NY - 1) + (NZ - 1))

    pending = []

    def send(stage, src, dst, device):
        copy = pltpu.make_async_remote_copy(
            src_ref=src, dst_ref=dst, send_sem=send_sem.at[stage], recv_sem=recv_sem.at[stage],
            device_id=device, device_id_type=MESH,
        )
        copy.start()
        return copy

    def spread_out(stage, name, source, buffer):
        n, me, peer = axes[name]
        for step in range(1, n):
            p = lax.rem(me + step, n)
            send(stage, source(p), buffer.at[me], peer(p))
        others = buffer.at[pl.ds(0, n - 1)]
        pending.append((stage, others))

    def arrived(stage, name, buffer):
        n = axes[name][0]
        others = buffer.at[pl.ds(0, n - 1)]
        pltpu.make_async_remote_copy(
            src_ref=others, dst_ref=others, send_sem=send_sem.at[stage],
            recv_sem=recv_sem.at[stage], device_id=sibling, device_id_type=MESH,
        ).wait_recv()

    meta_copy = send(META, meta.at[c], meta.at[c], sibling)
    rows_copy = send(
        ROWS, sens.at[:, :, pl.ds(pl.multiple_of((1 - c) * 512, 512), 512)], rows.at[c], sibling
    )
    meta_copy.wait_recv()

    cs_own[...] = meta[0, 1] + meta[1, 1]
    csz[z] = cs_own[...]
    csy[y] = cs_own[...]
    spread_out(CSY, "y", lambda p: cs_own, csy)
    spread_out(CSZ, "z", lambda p: cs_own, csz)

    raw = [meta[k, 0, 2:3, 0:32] for k in range(2)]
    keeps = [meta[k, 0, 3:4, 0:32] for k in range(2)]
    station_high = [
        meta[k, 0, 4:5, 0:32] == iota((8, 32), 0).astype(F32) for k in range(2)
    ]
    station_low = [
        (meta[k, 0, 5:6, 0:32] == iota((128, 32), 0).astype(F32)).astype(F32) for k in range(2)
    ]
    ray_of = lax.shift_right_logical(iota((256, 32), 0), 3) == iota((256, 32), 1)
    sub = iota((256, 128), 0)
    lane = iota((256, 128), 1)
    for k in range(2):
        column = jnp.zeros((256, 1), F32)
        for h in range(2):
            part = meta[k, 0, h : h + 1, :]
            ohr[k, :, 128 * h : 128 * h + 128] = (
                jnp.where(part == sub.astype(F32), 1.0, 0.0).astype(BF16)
            )
            column += jnp.sum(
                jnp.where(sub == lane + 128 * h, part, 0.0), axis=1, keepdims=True
            )
        for h in range(2):
            ohc[k, :, 128 * h : 128 * h + 128] = (
                jnp.where(column == (lane + 128 * h).astype(F32), 1.0, 0.0).astype(BF16)
            )

    own_rows.wait()
    rows_copy.wait_recv()

    def adjoint_and_reduce(it, ray):
        stage = 8 + 15 * it
        square = ray[0] * ray[0] + ray[1] * ray[1]
        stations = jnp.zeros((8, 128), F32)
        for k in range(2):
            stations += dot_nt(jnp.where(station_high[k], ray[k], 0.0), station_low[k])
        columns = [
            jnp.sum(jnp.where(ray_of, ray[k], 0.0), axis=1, keepdims=True) for k in range(2)
        ]
        for p in range(NX):
            sx[it, p, 16] = stations
            sx[it, p, 17] = jnp.zeros((8, 128), F32)
            sx[it, p, 17, 0:1, 0:32] = square

        def grad(half):
            result = None
            for k in range(2):
                part = rows[k, :, :, 256 * half : 256 * half + 256].reshape(256, 256)
                for piece in split(part * columns[k]):
                    term = dot(ohr[k], piece)
                    result = term if result is None else result + term
            return result

        value = grad(0)
        for p in range(NX):
            for j in range(2):
                sx[it, p, 8 * j : 8 * j + 8] = value[
                    64 * p : 64 * p + 64, 128 * j : 128 * j + 128
                ].reshape(8, 8, 128)
        spread_out(stage + S1X, "x", lambda p: sx.at[it, p], rx.at[it])
        value = grad(1)
        value_y = value[:, 0:128].reshape(NX, NY, 8, 128)
        value_z = value[:, 128:256].reshape(NX, NZ, 8, 128)
        for p in range(NY):
            sy[it, p] = value_y[:, p]
        spread_out(stage + S1Y, "y", lambda p: sy.at[it, p], ry.at[it])
        for p in range(NZ):
            sz[it, p] = value_z[:, p]
        spread_out(stage + S1Z, "z", lambda p: sz.at[it, p], rz.at[it])
        rx[it, x] = sx[it, x]
        ry[it, y] = sy[it, y]
        rz[it, z] = sz[it, z]

        def summed(buffer, n):
            result = buffer[it, 0]
            for p in range(1, n):
                result = result + buffer[it, p]
            return result

        if it == 0:
            arrived(CSY, "y", csy)
            cst[z] = csy[z]
            spread_out(CST, "z", lambda p: csy.at[p], cst)

        arrived(stage + S1X, "x", rx.at[it])
        sum_x = summed(rx, NX)
        for p in range(NY):
            s2y[it, p, 0] = sum_x[p]
            s2y[it, p, 1] = sum_x[16]
            s2y[it, p, 2] = sum_x[17]
        spread_out(stage + S2Y, "y", lambda p: s2y.at[it, p], r2y.at[it])
        for p in range(NZ):
            s2z[it, p, 0] = sum_x[8 + p]
        spread_out(stage + S2Z, "z", lambda p: s2z.at[it, p], r2z.at[it])
        r2y[it, y] = s2y[it, y]
        r2z[it, z] = s2z[it, z]

        arrived(stage + S1Y, "y", ry.at[it])
        sum_y = summed(ry, NY)
        for p in range(NX):
            s2x[it, p, 0] = sum_y[p]
        arrived(stage + S1Z, "z", rz.at[it])
        sum_z = summed(rz, NZ)
        for p in range(NX):
            s2x[it, p, 1] = sum_z[p]
        spread_out(stage + S2X, "x", lambda p: s2x.at[it, p], r2x.at[it])
        r2x[it, x] = s2x[it, x]

        arrived(stage + S2Y, "y", r2y.at[it])
        from_y = summed(r2y, NY)
        s3z[it, 0] = from_y[0]
        s3z[it, 2] = from_y[1]
        s3z[it, 3] = from_y[2]
        arrived(stage + S2Z, "z", r2z.at[it])
        s3y[it, 0] = summed(r2z, NZ)[0]
        arrived(stage + S2X, "x", r2x.at[it])
        from_x = summed(r2x, NX)
        s3z[it, 1] = from_x[0]
        s3y[it, 1] = from_x[1]
        spread_out(stage + S3Z, "z", lambda p: s3z.at[it], r3z.at[it])
        spread_out(stage + S3Y, "y", lambda p: s3y.at[it], r3y.at[it])
        r3z[it, z] = s3z[it]
        r3y[it, y] = s3y[it]
        arrived(stage + S3Z, "z", r3z.at[it])
        from_z = summed(r3z, NZ)
        arrived(stage + S3Y, "y", r3y.at[it])
        from_y = summed(r3y, NY)
        tiles = [from_z[0], from_y[0], from_z[1], from_y[1]]
        return tiles, from_z[2], jnp.sqrt(total(from_z[3]) + EPS)

    def gather(it, grads, scales):
        stage = 8 + 15 * it
        a2y[it, 0] = scales[0] * grads[0]
        a2y[it, 1] = grads[0] * grads[0] + grads[2] * grads[2]
        a2z[it, 0] = scales[1] * grads[1]
        a2z[it, 1] = grads[1] * grads[1] + grads[3] * grads[3]
        a2x[it, 0] = scales[2] * grads[2]
        a2x[it, 1] = scales[3] * grads[3]
        spread_out(stage + A2Y, "y", lambda p: a2y.at[it], g2y.at[it])
        spread_out(stage + A2Z, "z", lambda p: a2z.at[it], g2z.at[it])
        spread_out(stage + A2X, "x", lambda p: a2x.at[it], g2x.at[it])
        g2y[it, y] = a2y[it]
        g2z[it, z] = a2z[it]
        g2x[it, x] = a2x[it]
        arrived(stage + A2Y, "y", g2y.at[it])
        arrived(stage + A2Z, "z", g2z.at[it])
        square = None
        for p in range(NY):
            a1x[it, p] = g2y[it, p, 0]
            a1x[it, 8 + p] = g2z[it, p, 0]
            term = g2y[it, p, 1] + g2z[it, p, 1]
            square = term if square is None else square + term
        a1x[it, 16] = square
        spread_out(stage + A1X, "x", lambda p: a1x.at[it], gx.at[it])
        arrived(stage + A2X, "x", g2x.at[it])
        for p in range(NX):
            gy[it, y, p] = g2x[it, p, 0]
            gz[it, z, p] = g2x[it, p, 1]
        spread_out(stage + A1Y, "y", lambda p: gy.at[it, y], gy.at[it])
        spread_out(stage + A1Z, "z", lambda p: gz.at[it, z], gz.at[it])
        gx[it, x] = a1x[it]
        arrived(stage + A1X, "x", gx.at[it])
        square = gx[it, 0, 16]
        for p in range(1, NX):
            square = square + gx[it, p, 16]
        return square

    def forward(it, square):
        stage = 8 + 15 * it
        sums = [None, None]

        def add(half, values):
            pieces = split(values)
            for k in range(2):
                picked = dot(ohc[k], pieces[0]) + dot(ohc[k], pieces[1])
                part = rows[k, :, :, 256 * half : 256 * half + 256].reshape(256, 256) * picked
                part = part[:, 0:128] + part[:, 128:256]
                sums[k] = part if sums[k] is None else sums[k] + part

        add(
            0,
            jnp.concatenate(
                [gx[it, :, 0:8].reshape(256, 128), gx[it, :, 8:16].reshape(256, 128)], axis=1
            ),
        )
        arrived(stage + A1Y, "y", gy.at[it])
        arrived(stage + A1Z, "z", gz.at[it])
        add(
            1,
            jnp.concatenate(
                [
                    jnp.concatenate(
                        [buffer[it, :, p].reshape(64, 128) for p in range(NX)], axis=0
                    )
                    for buffer in (gy, gz)
                ],
                axis=1,
            ),
        )
        ex[it, c] = jnp.zeros((4, 8, 128), F32)
        for k in range(2):
            column = jnp.sum(sums[k], axis=1, keepdims=True)
            ex[it, c, 0, k : k + 1, 0:32] = jnp.sum(
                jnp.where(ray_of, column, 0.0), axis=0, keepdims=True
            )
        ex[it, c, 1] = square
        if it == 1:
            layer = lax.rem(z, 4)
            for i in range(2):
                ex[it, c, 2 + i] = jnp.where(
                    layer == 0,
                    gx[i, x, y],
                    jnp.where(
                        layer == 1, gx[i, x, 8 + y], jnp.where(layer == 2, gy[i, y, x], gz[i, y, x])
                    ),
                )
        copy = send(stage + EX, ex.at[it, c], ex.at[it, c], sibling)
        pending.append((stage + EX, ex.at[it, c]))
        copy.wait_recv()
        values = ex[it, 0, 0] + ex[it, 1, 0]
        return [values[k : k + 1, 0:32] for k in range(2)], total(ex[it, 0, 1] + ex[it, 1, 1])

    def station_values(stations):
        return [
            jnp.sum(
                jnp.where(
                    station_high[k],
                    jnp.dot(
                        stations, station_low[k], precision=HIGHEST, preferred_element_type=F32
                    ),
                    0.0,
                ),
                axis=0,
                keepdims=True,
            )
            for k in range(2)
        ]

    sums, station_sum, beta0 = adjoint_and_reduce(0, raw)
    unit = [raw[k] / beta0 for k in range(2)]
    arrived(CSZ, "z", csz)
    arrived(CST, "z", cst)
    first = 4 * c
    scales = [csz[first], cst[first + 1], csz[first + 2], cst[first + 3]]
    grads0 = [scales[j] * sums[j] / beta0 for j in range(4)]
    grad_station0 = station_sum / beta0
    square = gather(0, grads0, scales)
    product, model_square = forward(0, square)
    alpha0 = jnp.sqrt(model_square + total(grad_station0 * grad_station0) + EPS)
    dir_station0 = grad_station0 / alpha0

    at_station = station_values(dir_station0)
    raw = [
        keeps[k] * (product[k] / alpha0 + at_station[k]) - alpha0 * unit[k] for k in range(2)
    ]
    sums, station_sum, beta1 = adjoint_and_reduce(1, raw)
    unit = [raw[k] / beta1 for k in range(2)]
    grads1 = [scales[j] * sums[j] / beta1 - beta1 * (grads0[j] / alpha0) for j in range(4)]
    grad_station1 = station_sum / beta1 - beta1 * dir_station0
    square = gather(1, grads1, scales)
    product, model_square = forward(1, square)
    alpha1 = jnp.sqrt(model_square + total(grad_station1 * grad_station1) + EPS)
    dir_station1 = grad_station1 / alpha1
    rho = jnp.sqrt(alpha0 * alpha0 + beta1 * beta1)
    cosine = alpha0 / rho
    sine = beta1 / rho
    theta = sine * alpha1
    rho_bar = -cosine * alpha1
    step0 = cosine * beta0 / rho
    phi_bar = sine * beta0
    turn = theta / rho

    at_station = station_values(dir_station1)
    raw = [
        keeps[k] * (product[k] / alpha1 + at_station[k]) - alpha1 * unit[k] for k in range(2)
    ]
    fin[...] = jnp.zeros((3, 8, 128), F32)
    fin[0, 0:1, 0:32] = raw[0] * raw[0] + raw[1] * raw[1]
    spread_out(FX, "x", lambda p: fin.at[0], fx)
    fx[x] = fin[0]
    arrived(FX, "x", fx)
    fin[1] = jnp.sum(fx[...], axis=0)
    spread_out(FY, "y", lambda p: fin.at[1], fy)
    fy[y] = fin[1]
    arrived(FY, "y", fy)
    fin[2] = jnp.sum(fy[...], axis=0)
    spread_out(FZ, "z", lambda p: fin.at[2], fz)
    fz[z] = fin[2]
    arrived(FZ, "z", fz)
    beta2 = jnp.sqrt(total(jnp.sum(fz[...], axis=0)) + EPS)
    rho = jnp.sqrt(rho_bar * rho_bar + beta2 * beta2)
    step1 = rho_bar / rho * phi_bar / rho

    weight0 = (step0 - step1 * turn) / alpha0
    weight1 = step1 / alpha1
    holder = lax.div(z, 4)
    model = weight0 * ex[1, holder, 2] + weight1 * ex[1, holder, 3]
    out_model[0] = jnp.where(c == 0, model[0:4], model[4:8])
    out_station[...] = (step0 - step1 * turn) * dir_station0 + step1 * dir_station1
    out_ray[...] = jnp.where(c == 0, raw[0], raw[1]) / beta2

    meta_copy.wait_send()
    rows_copy.wait_send()
    for stage, others in pending:
        pltpu.make_async_remote_copy(
            src_ref=others, dst_ref=others, send_sem=send_sem.at[stage],
            recv_sem=recv_sem.at[stage], device_id=sibling, device_id_type=MESH,
        ).wait_send()


def per_device(sensitivity, owners, local_block, station_ids, kept, times, hit_counts):
    vmem = pl.BlockSpec(memory_space=pltpu.VMEM)

    def tiles(*shape):
        return pltpu.VMEM(shape + (8, 128), F32)

    model, station, ray = pl.pallas_call(
        kernel,
        out_shape=(
            jax.ShapeDtypeStruct((1, 4, 128), F32),
            jax.ShapeDtypeStruct((8, 128), F32),
            jax.ShapeDtypeStruct((1, 32), F32),
        ),
        in_specs=[pl.BlockSpec(memory_space=pl.ANY)] + [vmem] * 6,
        out_specs=(vmem,) * 3,
        scratch_shapes=[
            pltpu.VMEM((2, 32, 8, 512), F32),
            tiles(2, 2),
            pltpu.VMEM((2, 256, 256), BF16),
            pltpu.VMEM((2, 256, 256), BF16),
            tiles(), tiles(NZ), tiles(NY), tiles(NZ),
            tiles(3), tiles(NX), tiles(NY), tiles(NZ),
            tiles(2, NX, 18), tiles(2, NY, 4), tiles(2, NZ, 4),
            tiles(2, NX, 18), tiles(2, NY, 4), tiles(2, NZ, 4),
            tiles(2, NY, 3), tiles(2, NZ, 1), tiles(2, NX, 2),
            tiles(2, NY, 3), tiles(2, NZ, 1), tiles(2, NX, 2),
            tiles(2, 4), tiles(2, 2), tiles(2, NZ, 4), tiles(2, NY, 2),
            tiles(2, 2), tiles(2, 2), tiles(2, 2),
            tiles(2, NY, 2), tiles(2, NZ, 2), tiles(2, NX, 2),
            tiles(2, 17), tiles(2, NX, 17), tiles(2, NY, 4), tiles(2, NZ, 4),
            tiles(2, 2, 4),
            pltpu.SemaphoreType.DMA,
            pltpu.SemaphoreType.DMA((STAGES,)),
            pltpu.SemaphoreType.DMA((STAGES,)),
        ],
        compiler_params=pltpu.CompilerParams(
            collective_id=0, has_side_effects=True, vmem_limit_bytes=40 * 1024 * 1024
        ),
    )(
        sensitivity, owners, local_block, station_ids.reshape(1, 32), kept.reshape(1, 32),
        times.reshape(1, 32), hit_counts,
    )
    return model, station.reshape(1024), ray.reshape(32)


def solution(mesh):
    in_specs = (
        P(("depth", "block"), None, None),
        P(("depth", "block"), None),
        P(("depth", "block"), None),
        P(("depth", "block")),
        P(("depth", "block")),
        P(("depth", "block")),
        P("depth", "block", None),
    )
    out_specs = (P("depth", "block", None), P(), P(("depth", "block")))
    return jax.shard_map(
        per_device, mesh=mesh, in_specs=in_specs, out_specs=out_specs, check_vma=False
    )
```

```python
import functools

import jax
import jax.numpy as jnp
from jax import lax
from jax.experimental import pallas as pl
from jax.experimental.pallas import tpu as pltpu
from jax.sharding import PartitionSpec as P

NX, NY, NZ = 4, 8, 8
EPS = 1e-06
F32 = jnp.float32
BF16 = jnp.bfloat16
HIGHEST = lax.Precision.HIGHEST
MESH = pl.DeviceIdType.MESH

META, ROWS, CSZ, CSY, CST, FW, FZ, UNUSED = range(8)
S1X, S1Y, S1Z, S2Y, S2Z, S2X, S3Z, S3Y, A2Y, A2Z, A2X, A1X, A1Y, A1Z, EX = range(15)
STAGES = 8 + 2 * 15


def iota(shape, dim):
    return lax.broadcasted_iota(jnp.int32, shape, dim)


def total(tile):
    return jnp.sum(jnp.sum(tile, axis=0, keepdims=True), axis=1, keepdims=True)


def split(value):
    high = value.astype(BF16)
    return high, (value - high.astype(F32)).astype(BF16)


def dot(a, b):
    return jnp.dot(a, b, preferred_element_type=F32)


def dot_nt(a, b):
    return lax.dot_general(
        a, b, (((1,), (1,)), ((), ())), precision=HIGHEST, preferred_element_type=F32
    )


def kernel(
    sens, owners_in, local_in, station_in, kept_in, times_in, hits_in,
    out_model, out_station, out_ray,
    rows, meta, ohr, ohc, cs_own, csz, csy, cst, fin, fw, fz,
    sx, sy, sz, rx, ry, rz, s2y, s2z, s2x, r2y, r2z, r2x, s3z, s3y, r3z, r3y,
    a2y, a2z, a2x, g2y, g2z, g2x, a1x, gx, gy, gz, ex,
    owners, local_block, station_ids, kept, times, hits, local_sem, send_sem, recv_sem,
):
    z = lax.axis_index("depth")
    b = lax.axis_index("block")
    c = lax.rem(b, 2)
    y = lax.rem(lax.div(b, 2), NY)
    x = lax.div(b, 2 * NY)
    axes = {
        "x": (NX, x, lambda p: (z, (p * NY + y) * 2 + c)),
        "y": (NY, y, lambda p: (z, (x * NY + p) * 2 + c)),
        "z": (NZ, z, lambda p: (p, b)),
        "xy": (NX * NY, x * NY + y, lambda p: (z, p * 2 + c)),
    }
    sibling = (z, (x * NY + y) * 2 + 1 - c)

    own_rows = pltpu.make_async_copy(
        sens.at[:, :, pl.ds(pl.multiple_of(c * 512, 512), 512)], rows.at[c], local_sem.at[6]
    )
    fetches = [
        pltpu.make_async_copy(src, dst, local_sem.at[i])
        for i, (src, dst) in enumerate(
            (
                (owners_in, owners),
                (local_in, local_block),
                (station_in, station_ids),
                (kept_in, kept),
                (times_in, times),
                (hits_in, hits),
            )
        )
    ]
    for fetch in fetches:
        fetch.start()
    own_rows.start()

    barrier = pltpu.get_barrier_semaphore()
    pl.semaphore_signal(barrier, inc=1, device_id=sibling, device_id_type=MESH)
    for name in ("z", "xy"):
        n, me, peer = axes[name]
        for step in range(1, n):
            pl.semaphore_signal(
                barrier, inc=1, device_id=peer(lax.rem(me + step, n)), device_id_type=MESH
            )
    for fetch in fetches:
        fetch.wait()

    blocks = (owners[...] * 4 + local_block[...]).astype(F32)
    spread = (lax.shift_right_logical(iota((32, 256), 1), 3) == iota((32, 256), 0)).astype(F32)
    by_slot = jnp.dot(blocks, spread, precision=HIGHEST, preferred_element_type=F32)
    slot_of = jnp.bitwise_and(iota((8, 256), 1), 7)
    block_row = jnp.sum(
        jnp.where(iota((8, 256), 0) == slot_of, by_slot, 0.0), axis=0, keepdims=True
    )
    keep = kept[...].astype(F32)
    ids = station_ids[...]
    scale = 1.0 / jnp.sqrt(1.0 + hits[0].astype(F32))
    meta[c] = jnp.zeros((2, 8, 128), F32)
    meta[c, 0, 0:1, :] = block_row[:, 0:128]
    meta[c, 0, 1:2, :] = block_row[:, 128:256]
    meta[c, 0, 2:3, 0:32] = keep * times[...]
    meta[c, 0, 3:4, 0:32] = keep
    meta[c, 0, 4:5, 0:32] = lax.shift_right_logical(ids, 7).astype(F32)
    meta[c, 0, 5:6, 0:32] = jnp.bitwise_and(ids, 127).astype(F32)
    meta[c, 1, 0:4, :] = jnp.where(c == 0, scale, 0.0)
    meta[c, 1, 4:8, :] = jnp.where(c == 1, scale, 0.0)

    eye32 = iota((32, 32), 0) == iota((32, 32), 1)
    sub = iota((256, 128), 0)
    lane = iota((256, 128), 1)

    def one_hots(k, parts):
        column = jnp.zeros((256, 1), F32)
        for h in range(2):
            ohr[k, :, 128 * h : 128 * h + 128] = (
                jnp.where(parts[h] == sub.astype(F32), 1.0, 0.0).astype(BF16)
            )
            column += jnp.sum(
                jnp.where(sub == lane + 128 * h, parts[h], 0.0), axis=1, keepdims=True
            )
        for h in range(2):
            ohc[k, :, 128 * h : 128 * h + 128] = (
                jnp.where(column == (lane + 128 * h).astype(F32), 1.0, 0.0).astype(BF16)
            )

    one_hots(c, [block_row[:, 0:128], block_row[:, 128:256]])

    pl.semaphore_wait(barrier, 1 + (NX * NY - 1) + (NZ - 1))

    pending = []

    def send(stage, src, dst, device):
        copy = pltpu.make_async_remote_copy(
            src_ref=src, dst_ref=dst, send_sem=send_sem.at[stage], recv_sem=recv_sem.at[stage],
            device_id=device, device_id_type=MESH,
        )
        copy.start()
        return copy

    def spread_out(*parts):
        sends = []
        for stage, name, source, buffer in parts:
            n, me, peer = axes[name]
            for step in range(1, n):
                away = min(step, n - step)
                if name == "xy":
                    away = min(step // NY, NX - step // NY) + min(step % NY, NY - step % NY)
                sends.append((-away, len(sends), stage, name, source, buffer, step))
            pending.append((stage, buffer.at[pl.ds(0, n - 1)]))
        for away, order, stage, name, source, buffer, step in sorted(sends, key=lambda t: t[:2]):
            n, me, peer = axes[name]
            if name == "xy":
                p = lax.rem(x + step // NY, NX) * NY + lax.rem(y + step % NY, NY)
            else:
                p = lax.rem(me + step, n)
            send(stage, source(p), buffer.at[me], peer(p))

    def arrived(stage, name, buffer):
        n = axes[name][0]
        others = buffer.at[pl.ds(0, n - 1)]
        pltpu.make_async_remote_copy(
            src_ref=others, dst_ref=others, send_sem=send_sem.at[stage],
            recv_sem=recv_sem.at[stage], device_id=sibling, device_id_type=MESH,
        ).wait_recv()

    meta_copy = send(META, meta.at[c], meta.at[c], sibling)
    rows_copy = send(
        ROWS, sens.at[:, :, pl.ds(pl.multiple_of((1 - c) * 512, 512), 512)], rows.at[c], sibling
    )
    meta_copy.wait_recv()

    cs_own[...] = meta[0, 1] + meta[1, 1]
    csz[z] = cs_own[...]
    csy[y] = cs_own[...]
    spread_out((CSY, "y", lambda p: cs_own, csy), (CSZ, "z", lambda p: cs_own, csz))

    raw = [meta[k, 0, 2:3, 0:32] for k in range(2)]
    keeps = [meta[k, 0, 3:4, 0:32] for k in range(2)]
    station_high = [
        meta[k, 0, 4:5, 0:32] == iota((8, 32), 0).astype(F32) for k in range(2)
    ]
    station_low = [
        (meta[k, 0, 5:6, 0:32] == iota((128, 32), 0).astype(F32)).astype(F32) for k in range(2)
    ]
    one_hots(1 - c, [meta[1 - c, 0, h : h + 1, :] for h in range(2)])

    own_rows.wait()
    rows_copy.wait_recv()

    def adjoint_and_reduce(it, ray):
        stage = 8 + 15 * it
        square = ray[0] * ray[0] + ray[1] * ray[1]
        stations = jnp.zeros((8, 128), F32)
        for k in range(2):
            stations += dot_nt(jnp.where(station_high[k], ray[k], 0.0), station_low[k])
        columns = []
        for k in range(2):
            column = jnp.sum(jnp.where(eye32, ray[k], 0.0), axis=1, keepdims=True)
            column = jnp.broadcast_to(column, (32, 128)).reshape(32, 1, 128)
            column = jnp.broadcast_to(column, (32, 8, 128)).reshape(256, 128)
            columns.append(jnp.concatenate([column, column], axis=1))
        for p in range(NX):
            sx[it, p, 16] = stations
            sx[it, p, 17] = jnp.zeros((8, 128), F32)
            sx[it, p, 17, 0:1, 0:32] = square

        def grad(half):
            result = None
            for k in range(2):
                part = rows[k, :, :, 256 * half : 256 * half + 256].reshape(256, 256)
                for piece in split(part * columns[k]):
                    term = dot(ohr[k], piece)
                    result = term if result is None else result + term
            return result

        value = grad(0)
        for p in range(NX):
            for j in range(2):
                sx[it, p, 8 * j : 8 * j + 8] = value[
                    64 * p : 64 * p + 64, 128 * j : 128 * j + 128
                ].reshape(8, 8, 128)
        spread_out((stage + S1X, "x", lambda p: sx.at[it, p], rx.at[it]))
        value = grad(1)
        value_y = value[:, 0:128].reshape(NX, NY, 8, 128)
        value_z = value[:, 128:256].reshape(NX, NZ, 8, 128)
        for p in range(NY):
            sy[it, p] = value_y[:, p]
            sz[it, p] = value_z[:, p]
        spread_out(
            (stage + S1Y, "y", lambda p: sy.at[it, p], ry.at[it]),
            (stage + S1Z, "z", lambda p: sz.at[it, p], rz.at[it]),
        )
        rx[it, x] = sx[it, x]
        ry[it, y] = sy[it, y]
        rz[it, z] = sz[it, z]

        def summed(buffer, n):
            result = buffer[it, 0]
            for p in range(1, n):
                result = result + buffer[it, p]
            return result

        if it == 0:
            arrived(CSY, "y", csy)
            cst[z] = csy[z]
            spread_out((CST, "z", lambda p: csy.at[p], cst))

        arrived(stage + S1X, "x", rx.at[it])
        sum_x = summed(rx, NX)
        for p in range(NY):
            s2y[it, p, 0] = sum_x[p]
            s2y[it, p, 1] = sum_x[16]
            s2y[it, p, 2] = sum_x[17]
            s2z[it, p, 0] = sum_x[8 + p]
        spread_out(
            (stage + S2Y, "y", lambda p: s2y.at[it, p], r2y.at[it]),
            (stage + S2Z, "z", lambda p: s2z.at[it, p], r2z.at[it]),
        )
        r2y[it, y] = s2y[it, y]
        r2z[it, z] = s2z[it, z]

        arrived(stage + S1Y, "y", ry.at[it])
        sum_y = summed(ry, NY)
        for p in range(NX):
            s2x[it, p, 0] = sum_y[p]
        arrived(stage + S1Z, "z", rz.at[it])
        sum_z = summed(rz, NZ)
        for p in range(NX):
            s2x[it, p, 1] = sum_z[p]
        spread_out((stage + S2X, "x", lambda p: s2x.at[it, p], r2x.at[it]))
        r2x[it, x] = s2x[it, x]

        arrived(stage + S2Y, "y", r2y.at[it])
        from_y = summed(r2y, NY)
        s3z[it, 0] = from_y[0]
        s3z[it, 2] = from_y[1]
        s3z[it, 3] = from_y[2]
        arrived(stage + S2Z, "z", r2z.at[it])
        s3y[it, 0] = summed(r2z, NZ)[0]
        arrived(stage + S2X, "x", r2x.at[it])
        from_x = summed(r2x, NX)
        s3z[it, 1] = from_x[0]
        s3y[it, 1] = from_x[1]
        spread_out(
            (stage + S3Z, "z", lambda p: s3z.at[it], r3z.at[it]),
            (stage + S3Y, "y", lambda p: s3y.at[it], r3y.at[it]),
        )
        r3z[it, z] = s3z[it]
        r3y[it, y] = s3y[it]
        arrived(stage + S3Z, "z", r3z.at[it])
        from_z = summed(r3z, NZ)
        arrived(stage + S3Y, "y", r3y.at[it])
        from_y = summed(r3y, NY)
        tiles = [from_z[0], from_y[0], from_z[1], from_y[1]]
        return tiles, from_z[2], jnp.sqrt(total(from_z[3]) + EPS)

    def gather(it, grads, scales):
        stage = 8 + 15 * it
        a2y[it, 0] = scales[0] * grads[0]
        a2y[it, 1] = grads[0] * grads[0] + grads[2] * grads[2]
        a2z[it, 0] = scales[1] * grads[1]
        a2z[it, 1] = grads[1] * grads[1] + grads[3] * grads[3]
        a2x[it, 0] = scales[2] * grads[2]
        a2x[it, 1] = scales[3] * grads[3]
        spread_out(
            (stage + A2Y, "y", lambda p: a2y.at[it], g2y.at[it]),
            (stage + A2Z, "z", lambda p: a2z.at[it], g2z.at[it]),
            (stage + A2X, "x", lambda p: a2x.at[it], g2x.at[it]),
        )
        g2y[it, y] = a2y[it]
        g2z[it, z] = a2z[it]
        g2x[it, x] = a2x[it]
        arrived(stage + A2Y, "y", g2y.at[it])
        arrived(stage + A2Z, "z", g2z.at[it])
        square = None
        for p in range(NY):
            a1x[it, p] = g2y[it, p, 0]
            a1x[it, 8 + p] = g2z[it, p, 0]
            term = g2y[it, p, 1] + g2z[it, p, 1]
            square = term if square is None else square + term
        a1x[it, 16] = square
        spread_out((stage + A1X, "x", lambda p: a1x.at[it], gx.at[it]))
        arrived(stage + A2X, "x", g2x.at[it])
        for p in range(NX):
            gy[it, y, p] = g2x[it, p, 0]
            gz[it, z, p] = g2x[it, p, 1]
        spread_out(
            (stage + A1Y, "y", lambda p: gy.at[it, y], gy.at[it]),
            (stage + A1Z, "z", lambda p: gz.at[it, z], gz.at[it]),
        )
        gx[it, x] = a1x[it]
        arrived(stage + A1X, "x", gx.at[it])
        square = gx[it, 0, 16]
        for p in range(1, NX):
            square = square + gx[it, p, 16]
        return square

    def forward(it, square):
        stage = 8 + 15 * it
        sums = [None, None]

        def add(half, values):
            pieces = split(values)
            for k in range(2):
                picked = dot(ohc[k], pieces[0]) + dot(ohc[k], pieces[1])
                part = rows[k, :, :, 256 * half : 256 * half + 256].reshape(256, 256) * picked
                part = part[:, 0:128] + part[:, 128:256]
                sums[k] = part if sums[k] is None else sums[k] + part

        add(
            0,
            jnp.concatenate(
                [gx[it, :, 0:8].reshape(256, 128), gx[it, :, 8:16].reshape(256, 128)], axis=1
            ),
        )
        arrived(stage + A1Y, "y", gy.at[it])
        arrived(stage + A1Z, "z", gz.at[it])
        add(
            1,
            jnp.concatenate(
                [
                    jnp.concatenate(
                        [buffer[it, :, p].reshape(64, 128) for p in range(NX)], axis=0
                    )
                    for buffer in (gy, gz)
                ],
                axis=1,
            ),
        )
        ex[it, c] = jnp.zeros((4, 8, 128), F32)
        for k in range(2):
            column = jnp.sum(sums[k].reshape(32, 8, 128), axis=1)
            column = jnp.sum(column, axis=1, keepdims=True)
            ex[it, c, 0, k : k + 1, 0:32] = jnp.sum(
                jnp.where(eye32, column, 0.0), axis=0, keepdims=True
            )
        ex[it, c, 1] = square
        if it == 1:
            layer = lax.rem(z, 4)
            for i in range(2):
                ex[it, c, 2 + i] = jnp.where(
                    layer == 0,
                    gx[i, x, y],
                    jnp.where(
                        layer == 1, gx[i, x, 8 + y], jnp.where(layer == 2, gy[i, y, x], gz[i, y, x])
                    ),
                )
        copy = send(stage + EX, ex.at[it, c], ex.at[it, c], sibling)
        pending.append((stage + EX, ex.at[it, c]))
        copy.wait_recv()
        values = ex[it, 0, 0] + ex[it, 1, 0]
        return [values[k : k + 1, 0:32] for k in range(2)], total(ex[it, 0, 1] + ex[it, 1, 1])

    def station_values(stations):
        return [
            jnp.sum(
                jnp.where(
                    station_high[k],
                    jnp.dot(
                        stations, station_low[k], precision=HIGHEST, preferred_element_type=F32
                    ),
                    0.0,
                ),
                axis=0,
                keepdims=True,
            )
            for k in range(2)
        ]

    sums, station_sum, beta0 = adjoint_and_reduce(0, raw)
    unit = [raw[k] / beta0 for k in range(2)]
    arrived(CSZ, "z", csz)
    arrived(CST, "z", cst)
    first = 4 * c
    scales = [csz[first], cst[first + 1], csz[first + 2], cst[first + 3]]
    grads0 = [scales[j] * sums[j] / beta0 for j in range(4)]
    grad_station0 = station_sum / beta0
    square = gather(0, grads0, scales)
    product, model_square = forward(0, square)
    alpha0 = jnp.sqrt(model_square + total(grad_station0 * grad_station0) + EPS)
    dir_station0 = grad_station0 / alpha0

    at_station = station_values(dir_station0)
    raw = [
        keeps[k] * (product[k] / alpha0 + at_station[k]) - alpha0 * unit[k] for k in range(2)
    ]
    sums, station_sum, beta1 = adjoint_and_reduce(1, raw)
    unit = [raw[k] / beta1 for k in range(2)]
    grads1 = [scales[j] * sums[j] / beta1 - beta1 * (grads0[j] / alpha0) for j in range(4)]
    grad_station1 = station_sum / beta1 - beta1 * dir_station0
    square = gather(1, grads1, scales)
    product, model_square = forward(1, square)
    alpha1 = jnp.sqrt(model_square + total(grad_station1 * grad_station1) + EPS)
    dir_station1 = grad_station1 / alpha1
    rho = jnp.sqrt(alpha0 * alpha0 + beta1 * beta1)
    cosine = alpha0 / rho
    sine = beta1 / rho
    theta = sine * alpha1
    rho_bar = -cosine * alpha1
    step0 = cosine * beta0 / rho
    phi_bar = sine * beta0
    turn = theta / rho

    at_station = station_values(dir_station1)
    raw = [
        keeps[k] * (product[k] / alpha1 + at_station[k]) - alpha1 * unit[k] for k in range(2)
    ]
    fin[...] = jnp.zeros((2, 8, 128), F32)
    fin[0, 0:1, 0:32] = raw[0] * raw[0] + raw[1] * raw[1]
    spread_out((FW, "xy", lambda p: fin.at[0], fw))
    fw[x * NY + y] = fin[0]
    arrived(FW, "xy", fw)
    fin[1] = jnp.sum(fw[...], axis=0)
    spread_out((FZ, "z", lambda p: fin.at[1], fz))
    fz[z] = fin[1]
    arrived(FZ, "z", fz)
    beta2 = jnp.sqrt(total(jnp.sum(fz[...], axis=0)) + EPS)
    rho = jnp.sqrt(rho_bar * rho_bar + beta2 * beta2)
    step1 = rho_bar / rho * phi_bar / rho

    weight0 = (step0 - step1 * turn) / alpha0
    weight1 = step1 / alpha1
    holder = lax.div(z, 4)
    model = weight0 * ex[1, holder, 2] + weight1 * ex[1, holder, 3]
    out_model[0] = jnp.where(c == 0, model[0:4], model[4:8])
    out_station[...] = (step0 - step1 * turn) * dir_station0 + step1 * dir_station1
    out_ray[...] = jnp.where(c == 0, raw[0], raw[1]) / beta2

    meta_copy.wait_send()
    rows_copy.wait_send()
    for stage, others in pending:
        pltpu.make_async_remote_copy(
            src_ref=others, dst_ref=others, send_sem=send_sem.at[stage],
            recv_sem=recv_sem.at[stage], device_id=sibling, device_id_type=MESH,
        ).wait_send()


def hand_out(model, station, ray, out_model, out_station, out_ray, sem):
    copies = [
        pltpu.make_async_copy(src, dst, sem.at[i])
        for i, (src, dst) in enumerate(
            ((model, out_model), (station, out_station), (ray, out_ray))
        )
    ]
    for copy in copies:
        copy.start()
    for copy in copies:
        copy.wait()


def per_device(sensitivity, owners, local_block, station_ids, kept, times, hit_counts):
    vmem = pl.BlockSpec(memory_space=pltpu.VMEM)

    def tiles(*shape):
        return pltpu.VMEM(shape + (8, 128), F32)

    model, station, ray = pl.pallas_call(
        kernel,
        out_shape=(
            jax.ShapeDtypeStruct((1, 4, 128), F32),
            jax.ShapeDtypeStruct((8, 128), F32),
            jax.ShapeDtypeStruct((1, 32), F32),
        ),
        in_specs=[pl.BlockSpec(memory_space=pltpu.HBM)] * 7,
        out_specs=(vmem,) * 3,
        scratch_shapes=[
            pltpu.VMEM((2, 32, 8, 512), F32),
            tiles(2, 2),
            pltpu.VMEM((2, 256, 256), BF16),
            pltpu.VMEM((2, 256, 256), BF16),
            tiles(), tiles(NZ), tiles(NY), tiles(NZ),
            tiles(2), tiles(NX * NY), tiles(NZ),
            tiles(2, NX, 18), tiles(2, NY, 4), tiles(2, NZ, 4),
            tiles(2, NX, 18), tiles(2, NY, 4), tiles(2, NZ, 4),
            tiles(2, NY, 3), tiles(2, NZ, 1), tiles(2, NX, 2),
            tiles(2, NY, 3), tiles(2, NZ, 1), tiles(2, NX, 2),
            tiles(2, 4), tiles(2, 2), tiles(2, NZ, 4), tiles(2, NY, 2),
            tiles(2, 2), tiles(2, 2), tiles(2, 2),
            tiles(2, NY, 2), tiles(2, NZ, 2), tiles(2, NX, 2),
            tiles(2, 17), tiles(2, NX, 17), tiles(2, NY, 4), tiles(2, NZ, 4),
            tiles(2, 2, 4),
            pltpu.VMEM((8, 32), jnp.int32), pltpu.VMEM((8, 32), jnp.int32),
            pltpu.VMEM((1, 32), jnp.int32), pltpu.VMEM((1, 32), jnp.int32),
            pltpu.VMEM((1, 32), F32), pltpu.VMEM((1, 4, 128), jnp.int32),
            pltpu.SemaphoreType.DMA((7,)),
            pltpu.SemaphoreType.DMA((STAGES,)),
            pltpu.SemaphoreType.DMA((STAGES,)),
        ],
        compiler_params=pltpu.CompilerParams(
            collective_id=0, has_side_effects=True, vmem_limit_bytes=60 * 1024 * 1024
        ),
    )(
        sensitivity, owners.T, local_block.T, station_ids.reshape(1, 32), kept.reshape(1, 32),
        times.reshape(1, 32), hit_counts,
    )
    hbm = pl.BlockSpec(memory_space=pltpu.HBM)
    model, station, ray = pl.pallas_call(
        hand_out,
        out_shape=tuple(jax.ShapeDtypeStruct(a.shape, F32) for a in (model, station, ray)),
        in_specs=[hbm] * 3,
        out_specs=(hbm,) * 3,
        scratch_shapes=[pltpu.SemaphoreType.DMA((3,))],
    )(model, station, ray)
    return model, station.reshape(1024), ray.reshape(32)


def solution(mesh):
    in_specs = (
        P(("depth", "block"), None, None),
        P(("depth", "block"), None),
        P(("depth", "block"), None),
        P(("depth", "block")),
        P(("depth", "block")),
        P(("depth", "block")),
        P("depth", "block", None),
    )
    out_specs = (P("depth", "block", None), P(), P(("depth", "block")))
    return jax.shard_map(
        per_device, mesh=mesh, in_specs=in_specs, out_specs=out_specs, check_vma=False
    )
```

```python
import functools

import jax
import jax.numpy as jnp
from jax import lax
from jax.experimental import pallas as pl
from jax.experimental.pallas import tpu as pltpu
from jax.sharding import PartitionSpec as P

NX, NY, NZ = 4, 8, 8
EPS = 1e-06
F32 = jnp.float32
BF16 = jnp.bfloat16
HIGHEST = lax.Precision.HIGHEST
MESH = pl.DeviceIdType.MESH

ROWS = 0
META, CSZ, CSY, CST, FY, FZ = range(8, 14)
S1Y, S1Z, S2Z, S2Y, A1Y, A1Z, EX = range(7)
FIRST = 14
STAGES = FIRST + 2 * 7


def iota(shape, dim):
    return lax.broadcasted_iota(jnp.int32, shape, dim)


def total(tile):
    return jnp.sum(jnp.sum(tile, axis=0, keepdims=True), axis=1, keepdims=True)


def split(value):
    high = value.astype(BF16)
    return jnp.concatenate([high, (value - high.astype(F32)).astype(BF16)], axis=1)


def joined(value):
    return value[:, 0:128] + value[:, 128:256]


def dot(a, b):
    return jnp.dot(a, b, preferred_element_type=F32)


def dot_exact(a, b):
    return jnp.dot(a, b, precision=HIGHEST, preferred_element_type=F32)


def dot_nt(a, b):
    return lax.dot_general(
        a, b, (((1,), (1,)), ((), ())), precision=HIGHEST, preferred_element_type=F32
    )


def kernel(
    sens, owners_in, local_in, station_in, kept_in, times_in, hits_in,
    out_model, out_station, out_ray,
    rows, meta, ohr, ohc, cs_near, csz, csy, cst, fin, fy, fz,
    sy, sz, ry, rz, s2z, s2y, r2z, r2y, a1y, a1z, gy, gz, exs, ex,
    owners, local_block, station_ids, kept, times, hits, local_sem, send_sem, recv_sem,
):
    z = lax.axis_index("depth")
    b = lax.axis_index("block")
    c = lax.rem(b, 2)
    y = lax.rem(lax.div(b, 2), NY)
    x = lax.div(b, 2 * NY)
    q = x * 2 + c
    axes = {
        "y": (NY, y, lambda p: (z, (x * NY + p) * 2 + c)),
        "z": (NZ, z, lambda p: (p, b)),
        "g": (2 * NX, q, lambda p: (z, (lax.div(p, 2) * NY + y) * 2 + lax.rem(p, 2))),
    }

    def member(step, sign=1):
        return lax.rem(x + sign * (step // 2) + NX, NX) * 2 + lax.rem(c + step, 2)

    fetches = [
        pltpu.make_async_copy(src, dst, local_sem.at[i])
        for i, (src, dst) in enumerate(
            (
                (owners_in, owners),
                (local_in, local_block),
                (station_in, station_ids),
                (kept_in, kept),
                (times_in, times),
                (hits_in, hits),
            )
        )
    ]
    for fetch in fetches:
        fetch.start()

    def layer_of_rows(p):
        return sens.at[:, :, pl.ds(pl.multiple_of(p * 128, 128), 128)]

    own_rows = pltpu.make_async_copy(layer_of_rows(q), rows.at[q], local_sem.at[6])
    own_rows.start()

    barrier = pltpu.get_barrier_semaphore()
    for name in "yz":
        n, me, peer = axes[name]
        for step in (4, 3, 5, 2, 6, 1, 7):
            pl.semaphore_signal(
                barrier, inc=1, device_id=peer(lax.rem(me + step, n)), device_id_type=MESH
            )
    for step in (4, 5, 2, 3, 6, 7, 1):
        pl.semaphore_signal(
            barrier, inc=1, device_id=axes["g"][2](member(step)), device_id_type=MESH
        )
    for fetch in fetches:
        fetch.wait()

    blocks = (owners[...] * 4 + local_block[...]).astype(F32)
    widen = (lax.shift_right_logical(iota((32, 256), 1), 3) == iota((32, 256), 0)).astype(F32)
    by_slot = dot_exact(blocks, widen)
    slot_of = jnp.bitwise_and(iota((8, 256), 1), 7)
    block_row = jnp.sum(
        jnp.where(iota((8, 256), 0) == slot_of, by_slot, 0.0), axis=0, keepdims=True
    )
    keep = kept[...].astype(F32)
    kind = iota((8, 32), 0)
    stacked = jnp.where(
        kind < 4, keep * times[...], jnp.where(kind < 6, keep, station_ids[...].astype(F32))
    )
    repeat = (jnp.bitwise_and(iota((32, 128), 1), 31) == iota((32, 128), 0)).astype(F32)
    mine = jnp.logical_and(
        lax.shift_right_logical(iota((8, 128), 1), 5) == lax.rem(q, 4),
        jnp.bitwise_and(iota((8, 128), 0), 1) == lax.div(q, 4),
    )
    scale = 1.0 / jnp.sqrt(1.0 + hits[0].astype(F32))
    meta[q, 0] = jnp.where(mine, dot_exact(stacked, repeat), 0.0)
    meta[q, 0, 0:1, :] = block_row[:, 0:128]
    meta[q, 0, 1:2, :] = block_row[:, 128:256]
    meta[q, 1, 0:4, :] = jnp.where(c == 0, scale, 0.0)
    meta[q, 1, 4:8, :] = jnp.where(c == 1, scale, 0.0)

    pl.semaphore_wait(barrier, 7 + (NY - 1) + (NZ - 1))

    pending = []

    def send(stage, src, dst, device):
        copy = pltpu.make_async_remote_copy(
            src_ref=src, dst_ref=dst, send_sem=send_sem.at[stage], recv_sem=recv_sem.at[stage],
            device_id=device, device_id_type=MESH,
        )
        copy.start()
        return copy

    def spread_out(*parts):
        sends = []
        for stage, name, source, buffer in parts:
            n, me, peer = axes[name]
            for step in range(1, n):
                away = min(step, n - step)
                if name == "g":
                    away = min(step // 2, NX - step // 2)
                sends.append((-away, len(sends), stage, name, source, buffer, step))
            pending.append((stage, buffer.at[pl.ds(0, n - 1)]))
        for away, order, stage, name, source, buffer, step in sorted(sends, key=lambda t: t[:2]):
            n, me, peer = axes[name]
            p = member(step) if name == "g" else lax.rem(me + step, n)
            send(stage, source(p), buffer.at[me], peer(p))

    def arrived(stage, name, buffer):
        n, me, peer = axes[name]
        others = buffer.at[pl.ds(0, n - 1)]
        pltpu.make_async_remote_copy(
            src_ref=others, dst_ref=others, send_sem=send_sem.at[stage],
            recv_sem=recv_sem.at[stage], device_id=peer(lax.rem(me + 1, n)), device_id_type=MESH,
        ).wait_recv()

    spread_out((META, "g", lambda p: meta.at[q], meta))
    row_copies = {}
    for step in (1, 4, 5, 2, 3, 6, 7):
        p = member(step)
        row_copies[step] = send(ROWS + step, layer_of_rows(p), rows.at[q], axes["g"][2](p))
    arrived(META, "g", meta)

    for i in range(NX):
        cs_near[i] = meta[2 * i, 1] + meta[2 * i + 1, 1]
    csz[z] = cs_near[0:2]
    csy[y] = cs_near[2:4]
    spread_out(
        (CSY, "y", lambda p: cs_near.at[pl.ds(2, 2)], csy),
        (CSZ, "z", lambda p: cs_near.at[pl.ds(0, 2)], csz),
    )

    packed = meta[0, 0]
    for k in range(1, 8):
        packed = packed + meta[k, 0]
    raw = [packed[2 + h : 3 + h] for h in range(2)]
    keeps = [packed[4 + h : 5 + h] for h in range(2)]
    ids = [packed[6 + h : 7 + h].astype(jnp.int32) for h in range(2)]
    station_high = [
        lax.shift_right_logical(ids[h], 7) == iota((8, 128), 0) for h in range(2)
    ]
    station_low = [
        (jnp.bitwise_and(ids[h], 127) == iota((128, 128), 0)).astype(F32) for h in range(2)
    ]
    sub = iota((256, 128), 0)
    lane = iota((256, 128), 1)
    for k in range(8):
        column = jnp.zeros((256, 1), F32)
        for h in range(2):
            part = meta[k, 0, h : h + 1, :]
            ohr[k, :, 128 * h : 128 * h + 128] = (
                jnp.where(part == sub.astype(F32), 1.0, 0.0).astype(BF16)
            )
            column += jnp.sum(
                jnp.where(sub == lane + 128 * h, part, 0.0), axis=1, keepdims=True
            )
        for h in range(2):
            ohc[k, :, 128 * h : 128 * h + 128] = (
                jnp.where(column == (lane + 128 * h).astype(F32), 1.0, 0.0).astype(BF16)
            )

    def lanes_of(k):
        return iota((32, 128), 1) == iota((32, 128), 0) + 32 * lax.rem(k, 4)

    def column_of(k, ray):
        half = jnp.where(k < 4, ray[0], ray[1])
        return jnp.sum(jnp.where(lanes_of(k), half, 0.0), axis=1, keepdims=True)

    def summed(buffer, it, n):
        result = buffer[it, 0]
        for p in range(1, n):
            result = result + buffer[it, p]
        return result

    def adjoint_and_reduce(it, ray):
        stage = FIRST + 7 * it
        stations = jnp.zeros((8, 128), F32)
        for h in range(2):
            stations += dot_nt(jnp.where(station_high[h], ray[h], 0.0), station_low[h])
        for p in range(NY):
            sy[it, p, 2] = stations
            sy[it, p, 3] = jnp.zeros((8, 128), F32)
            for h in range(2):
                sy[it, p, 3, h : h + 1, :] = ray[h] * ray[h]
        value = None
        for step in (0, 1, 2, 3, 6, 7, 4, 5):
            k = member(step, -1)
            if it == 0:
                if step:
                    row_copies[step].wait_recv()
                else:
                    own_rows.wait()
            column = jnp.broadcast_to(column_of(k, ray), (32, 128)).reshape(32, 1, 128)
            term = dot(ohr[k], split((rows[k] * column).reshape(256, 128)))
            value = term if value is None else value + term
        value = joined(value).reshape(NX, NY, 8, 128)
        for p in range(NY):
            for i in range(2):
                sy[it, p, i] = value[i, p]
                sz[it, p, i] = value[2 + i, p]
        spread_out(
            (stage + S1Y, "y", lambda p: sy.at[it, p], ry.at[it]),
            (stage + S1Z, "z", lambda p: sz.at[it, p], rz.at[it]),
        )
        ry[it, y] = sy[it, y]
        rz[it, z] = sz[it, z]
        if it == 0:
            arrived(CSY, "y", csy)
            cst[z] = csy[z]
            spread_out((CST, "z", lambda p: csy.at[p], cst))
        arrived(stage + S1Y, "y", ry.at[it])
        s2z[it] = summed(ry, it, NY)
        spread_out((stage + S2Z, "z", lambda p: s2z.at[it], r2z.at[it]))
        arrived(stage + S1Z, "z", rz.at[it])
        s2y[it] = summed(rz, it, NZ)
        spread_out((stage + S2Y, "y", lambda p: s2y.at[it], r2y.at[it]))
        r2z[it, z] = s2z[it]
        r2y[it, y] = s2y[it]
        arrived(stage + S2Z, "z", r2z.at[it])
        from_z = summed(r2z, it, NZ)
        arrived(stage + S2Y, "y", r2y.at[it])
        from_y = summed(r2y, it, NY)
        return [from_z[0:2], from_y], from_z[2], jnp.sqrt(total(from_z[3]) + EPS)

    def gather(it, grads, scales):
        stage = FIRST + 7 * it
        for buffer, grad, scale in ((a1y, grads[0], scales[0]), (a1z, grads[1], scales[1])):
            buffer[it, 0:2] = scale * grad
            buffer[it, 2] = grad[0] * grad[0] + grad[1] * grad[1]
        spread_out(
            (stage + A1Y, "y", lambda p: a1y.at[it], gy.at[it]),
            (stage + A1Z, "z", lambda p: a1z.at[it], gz.at[it]),
        )
        gy[it, y] = a1y[it]
        gz[it, z] = a1z[it]

    def forward(it):
        stage = FIRST + 7 * it
        arrived(stage + A1Y, "y", gy.at[it])
        arrived(stage + A1Z, "z", gz.at[it])
        values = split(
            jnp.concatenate(
                [buffer[it, :, i].reshape(64, 128) for buffer in (gy, gz) for i in range(2)],
                axis=0,
            )
        )
        halves = [jnp.zeros((1, 128), F32), jnp.zeros((1, 128), F32)]
        for k in range(8):
            part = rows[k].reshape(256, 128) * joined(dot(ohc[k], values))
            column = jnp.sum(part.reshape(32, 8, 128), axis=1)
            column = jnp.sum(column, axis=1, keepdims=True)
            halves[k // 4] += jnp.sum(jnp.where(lanes_of(k), column, 0.0), axis=0, keepdims=True)
        square = gy[it, 0, 2] + gz[it, 0, 2]
        for p in range(1, NY):
            square = square + (gy[it, p, 2] + gz[it, p, 2])
        for p in range(8):
            exs[it, p, 0] = jnp.zeros((8, 128), F32)
            for h in range(2):
                exs[it, p, 0, h : h + 1, :] = halves[h]
            exs[it, p, 1] = square
            for i in range(2):
                if it == 1:
                    exs[it, p, 2 + i] = (gy if p < 4 else gz)[i, y, p // 2 % 2]
        width = 4 if it == 1 else 2
        spread_out(
            (
                stage + EX,
                "g",
                lambda p: exs.at[it, p, pl.ds(0, width)],
                ex.at[it, :, pl.ds(0, width)],
            )
        )
        ex[it, q, 0:width] = exs[it, q, 0:width]
        arrived(stage + EX, "g", ex.at[it, :, pl.ds(0, width)])
        value = ex[it, 0, 0:2]
        for k in range(1, 8):
            value = value + ex[it, k, 0:2]
        return [value[0, h : h + 1] for h in range(2)], total(value[1])

    def station_values(stations):
        return [
            jnp.sum(
                jnp.where(station_high[h], dot_exact(stations, station_low[h]), 0.0),
                axis=0,
                keepdims=True,
            )
            for h in range(2)
        ]

    sums, station_sum, beta0 = adjoint_and_reduce(0, raw)
    unit = [raw[h] / beta0 for h in range(2)]
    arrived(CSZ, "z", csz)
    arrived(CST, "z", cst)
    scales = [csz[q], cst[q]]
    grads0 = [scales[j] * sums[j] / beta0 for j in range(2)]
    grad_station0 = station_sum / beta0
    gather(0, grads0, scales)
    product, model_square = forward(0)
    alpha0 = jnp.sqrt(model_square + total(grad_station0 * grad_station0) + EPS)
    dir_station0 = grad_station0 / alpha0

    at_station = station_values(dir_station0)
    raw = [
        keeps[h] * (product[h] / alpha0 + at_station[h]) - alpha0 * unit[h] for h in range(2)
    ]
    sums, station_sum, beta1 = adjoint_and_reduce(1, raw)
    unit = [raw[h] / beta1 for h in range(2)]
    grads1 = [scales[j] * sums[j] / beta1 - beta1 * (grads0[j] / alpha0) for j in range(2)]
    grad_station1 = station_sum / beta1 - beta1 * dir_station0
    gather(1, grads1, scales)
    product, model_square = forward(1)
    alpha1 = jnp.sqrt(model_square + total(grad_station1 * grad_station1) + EPS)
    dir_station1 = grad_station1 / alpha1
    rho = jnp.sqrt(alpha0 * alpha0 + beta1 * beta1)
    cosine = alpha0 / rho
    sine = beta1 / rho
    theta = sine * alpha1
    rho_bar = -cosine * alpha1
    step0 = cosine * beta0 / rho
    phi_bar = sine * beta0
    turn = theta / rho

    at_station = station_values(dir_station1)
    raw = [
        keeps[h] * (product[h] / alpha1 + at_station[h]) - alpha1 * unit[h] for h in range(2)
    ]
    fin[...] = jnp.zeros((2, 8, 128), F32)
    for h in range(2):
        fin[0, h : h + 1, :] = raw[h] * raw[h]
    spread_out((FY, "y", lambda p: fin.at[0], fy))
    fy[y] = fin[0]
    arrived(FY, "y", fy)
    fin[1] = jnp.sum(fy[...], axis=0)
    spread_out((FZ, "z", lambda p: fin.at[1], fz))
    fz[z] = fin[1]
    own_ray = jnp.sum(
        jnp.where(iota((32, 32), 0) == iota((32, 32), 1), column_of(q, raw), 0.0),
        axis=0,
        keepdims=True,
    )
    arrived(FZ, "z", fz)
    beta2 = jnp.sqrt(total(jnp.sum(fz[...], axis=0)) + EPS)
    rho = jnp.sqrt(rho_bar * rho_bar + beta2 * beta2)
    step1 = rho_bar / rho * phi_bar / rho

    weight0 = (step0 - step1 * turn) / alpha0
    weight1 = step1 / alpha1
    model = weight0 * ex[1, z, 2] + weight1 * ex[1, z, 3]
    out_model[0] = jnp.where(c == 0, model[0:4], model[4:8])
    out_station[...] = (step0 - step1 * turn) * dir_station0 + step1 * dir_station1
    out_ray[...] = own_ray / beta2

    for step in row_copies:
        row_copies[step].wait_send()
    for stage, others in pending:
        pltpu.make_async_remote_copy(
            src_ref=others, dst_ref=others, send_sem=send_sem.at[stage],
            recv_sem=recv_sem.at[stage], device_id=axes["g"][2](member(1)), device_id_type=MESH,
        ).wait_send()


def hand_out(model, station, ray, out_model, out_station, out_ray, sem):
    copies = [
        pltpu.make_async_copy(src, dst, sem.at[i])
        for i, (src, dst) in enumerate(
            ((model, out_model), (station, out_station), (ray, out_ray))
        )
    ]
    for copy in copies:
        copy.start()
    for copy in copies:
        copy.wait()


def per_device(sensitivity, owners, local_block, station_ids, kept, times, hit_counts):
    vmem = pl.BlockSpec(memory_space=pltpu.VMEM)

    def tiles(*shape):
        return pltpu.VMEM(shape + (8, 128), F32)

    model, station, ray = pl.pallas_call(
        kernel,
        out_shape=(
            jax.ShapeDtypeStruct((1, 4, 128), F32),
            jax.ShapeDtypeStruct((8, 128), F32),
            jax.ShapeDtypeStruct((1, 32), F32),
        ),
        in_specs=[pl.BlockSpec(memory_space=pltpu.HBM)] * 7,
        out_specs=(vmem,) * 3,
        scratch_shapes=[
            pltpu.VMEM((8, 32, 8, 128), F32),
            tiles(8, 2),
            pltpu.VMEM((8, 256, 256), BF16),
            pltpu.VMEM((8, 256, 256), BF16),
            tiles(NX), tiles(NZ, 2), tiles(NY, 2), tiles(NZ, 2),
            tiles(2), tiles(NY), tiles(NZ),
            tiles(2, NY, 4), tiles(2, NZ, 2), tiles(2, NY, 4), tiles(2, NZ, 2),
            tiles(2, 4), tiles(2, 2), tiles(2, NZ, 4), tiles(2, NY, 2),
            tiles(2, 3), tiles(2, 3), tiles(2, NY, 3), tiles(2, NZ, 3),
            tiles(2, 8, 4), tiles(2, 8, 4),
            pltpu.VMEM((8, 32), jnp.int32), pltpu.VMEM((8, 32), jnp.int32),
            pltpu.VMEM((1, 32), jnp.int32), pltpu.VMEM((1, 32), jnp.int32),
            pltpu.VMEM((1, 32), F32), pltpu.VMEM((1, 4, 128), jnp.int32),
            pltpu.SemaphoreType.DMA((7,)),
            pltpu.SemaphoreType.DMA((STAGES,)),
            pltpu.SemaphoreType.DMA((STAGES,)),
        ],
        compiler_params=pltpu.CompilerParams(
            collective_id=0, has_side_effects=True, vmem_limit_bytes=60 * 1024 * 1024
        ),
    )(
        sensitivity, owners.T, local_block.T, station_ids.reshape(1, 32), kept.reshape(1, 32),
        times.reshape(1, 32), hit_counts,
    )
    hbm = pl.BlockSpec(memory_space=pltpu.HBM)
    model, station, ray = pl.pallas_call(
        hand_out,
        out_shape=tuple(jax.ShapeDtypeStruct(a.shape, F32) for a in (model, station, ray)),
        in_specs=[hbm] * 3,
        out_specs=(hbm,) * 3,
        scratch_shapes=[pltpu.SemaphoreType.DMA((3,))],
    )(model, station, ray)
    return model, station.reshape(1024), ray.reshape(32)


def solution(mesh):
    in_specs = (
        P(("depth", "block"), None, None),
        P(("depth", "block"), None),
        P(("depth", "block"), None),
        P(("depth", "block")),
        P(("depth", "block")),
        P(("depth", "block")),
        P("depth", "block", None),
    )
    out_specs = (P("depth", "block", None), P(), P(("depth", "block")))
    return jax.shard_map(
        per_device, mesh=mesh, in_specs=in_specs, out_specs=out_specs, check_vma=False
    )
```

```python
import functools

import jax
import jax.numpy as jnp
from jax import lax
from jax.experimental import pallas as pl
from jax.experimental.pallas import tpu as pltpu
from jax.sharding import PartitionSpec as P

NX, NY, NZ = 4, 8, 8
EPS = 1e-06
F32 = jnp.float32
BF16 = jnp.bfloat16
HIGHEST = lax.Precision.HIGHEST
MESH = pl.DeviceIdType.MESH

ROWS = 0
META, CSZ, CSY, CST, FY, FZ = range(8, 14)
S1Y, S1Z, S2Z, S2Y, A1Y, A1Z, EX = range(7)
FIRST = 14
STAGES = FIRST + 2 * 7


def iota(shape, dim):
    return lax.broadcasted_iota(jnp.int32, shape, dim)


def total(tile):
    return jnp.sum(jnp.sum(tile, axis=0, keepdims=True), axis=1, keepdims=True)


def split(value):
    high = value.astype(BF16)
    return jnp.concatenate([high, (value - high.astype(F32)).astype(BF16)], axis=1)


def joined(value):
    return value[:, 0:128] + value[:, 128:256]


def dot(a, b):
    return jnp.dot(a, b, preferred_element_type=F32)


def dot_exact(a, b):
    return jnp.dot(a, b, precision=HIGHEST, preferred_element_type=F32)


def dot_nt(a, b):
    return lax.dot_general(
        a, b, (((1,), (1,)), ((), ())), precision=HIGHEST, preferred_element_type=F32
    )


def kernel(
    sens, owners_in, local_in, station_in, kept_in, times_in, hits_in,
    out_model, out_station, out_ray,
    rows, parcels, meta, ohr, ohc, cs_near, csz, csy, cst, fin, fy, fz,
    sy, sz, ry, rz, s2z, s2y, r2z, r2y, a1y, a1z, gy, gz, exs, ex,
    owners, local_block, station_ids, kept, times, hits, local_sem, send_sem, recv_sem,
):
    z = lax.axis_index("depth")
    b = lax.axis_index("block")
    c = lax.rem(b, 2)
    y = lax.rem(lax.div(b, 2), NY)
    x = lax.div(b, 2 * NY)
    q = x * 2 + c
    axes = {
        "y": (NY, y, lambda p: (z, (x * NY + p) * 2 + c)),
        "z": (NZ, z, lambda p: (p, b)),
        "g": (2 * NX, q, lambda p: (z, (lax.div(p, 2) * NY + y) * 2 + lax.rem(p, 2))),
    }

    def member(step, sign=1):
        return lax.rem(x + sign * (step // 2) + NX, NX) * 2 + lax.rem(c + step, 2)

    fetches = [
        pltpu.make_async_copy(src, dst, local_sem.at[i])
        for i, (src, dst) in enumerate(
            (
                (owners_in, owners),
                (local_in, local_block),
                (station_in, station_ids),
                (kept_in, kept),
                (times_in, times),
                (hits_in, hits),
            )
        )
    ]
    for fetch in fetches:
        fetch.start()

    def layer_of_rows(p):
        return sens.at[:, :, pl.ds(pl.multiple_of(p * 128, 128), 128)]

    own_rows = pltpu.make_async_copy(layer_of_rows(q), rows.at[q], local_sem.at[6])
    own_rows.start()
    packings = [
        pltpu.make_async_copy(layer_of_rows(p), parcels.at[p], local_sem.at[7 + p])
        for p in range(8)
    ]
    for packing in packings:
        packing.start()

    barrier = pltpu.get_barrier_semaphore()
    for name in "yz":
        n, me, peer = axes[name]
        for step in (4, 3, 5, 2, 6, 1, 7):
            pl.semaphore_signal(
                barrier, inc=1, device_id=peer(lax.rem(me + step, n)), device_id_type=MESH
            )
    for step in (4, 5, 2, 3, 6, 7, 1):
        pl.semaphore_signal(
            barrier, inc=1, device_id=axes["g"][2](member(step)), device_id_type=MESH
        )
    for fetch in fetches + packings:
        fetch.wait()

    blocks = (owners[...] * 4 + local_block[...]).astype(F32)
    widen = (lax.shift_right_logical(iota((32, 256), 1), 3) == iota((32, 256), 0)).astype(F32)
    by_slot = dot_exact(blocks, widen)
    slot_of = jnp.bitwise_and(iota((8, 256), 1), 7)
    block_row = jnp.sum(
        jnp.where(iota((8, 256), 0) == slot_of, by_slot, 0.0), axis=0, keepdims=True
    )
    keep = kept[...].astype(F32)
    kind = iota((8, 32), 0)
    stacked = jnp.where(
        kind < 4, keep * times[...], jnp.where(kind < 6, keep, station_ids[...].astype(F32))
    )
    repeat = (jnp.bitwise_and(iota((32, 128), 1), 31) == iota((32, 128), 0)).astype(F32)
    mine = jnp.logical_and(
        lax.shift_right_logical(iota((8, 128), 1), 5) == lax.rem(q, 4),
        jnp.bitwise_and(iota((8, 128), 0), 1) == lax.div(q, 4),
    )
    scale = 1.0 / jnp.sqrt(1.0 + hits[0].astype(F32))
    meta[q, 0] = jnp.where(mine, dot_exact(stacked, repeat), 0.0)
    meta[q, 0, 0:1, :] = block_row[:, 0:128]
    meta[q, 0, 1:2, :] = block_row[:, 128:256]
    meta[q, 1, 0:4, :] = jnp.where(c == 0, scale, 0.0)
    meta[q, 1, 4:8, :] = jnp.where(c == 1, scale, 0.0)

    pl.semaphore_wait(barrier, 7 + (NY - 1) + (NZ - 1))

    pending = []

    def send(stage, src, dst, device):
        copy = pltpu.make_async_remote_copy(
            src_ref=src, dst_ref=dst, send_sem=send_sem.at[stage], recv_sem=recv_sem.at[stage],
            device_id=device, device_id_type=MESH,
        )
        copy.start()
        return copy

    def spread_out(*parts):
        sends = []
        for stage, name, source, buffer in parts:
            n, me, peer = axes[name]
            for step in range(1, n):
                away = min(step, n - step)
                if name == "g":
                    away = min(step // 2, NX - step // 2)
                sends.append((-away, len(sends), stage, name, source, buffer, step))
            pending.append((stage, buffer.at[pl.ds(0, n - 1)]))
        for away, order, stage, name, source, buffer, step in sorted(sends, key=lambda t: t[:2]):
            n, me, peer = axes[name]
            p = member(step) if name == "g" else lax.rem(me + step, n)
            send(stage, source(p), buffer.at[me], peer(p))

    def arrived(stage, name, buffer):
        n, me, peer = axes[name]
        others = buffer.at[pl.ds(0, n - 1)]
        pltpu.make_async_remote_copy(
            src_ref=others, dst_ref=others, send_sem=send_sem.at[stage],
            recv_sem=recv_sem.at[stage], device_id=peer(lax.rem(me + 1, n)), device_id_type=MESH,
        ).wait_recv()

    spread_out((META, "g", lambda p: meta.at[q], meta))
    row_copies = {}
    for step in (1, 2, 6, 3, 7, 4, 5):
        p = member(step)
        row_copies[step] = send(ROWS + step, parcels.at[p], rows.at[q], axes["g"][2](p))
    arrived(META, "g", meta)

    for i in range(NX):
        cs_near[i] = meta[2 * i, 1] + meta[2 * i + 1, 1]
    csz[z] = cs_near[0:2]
    csy[y] = cs_near[2:4]
    spread_out(
        (CSY, "y", lambda p: cs_near.at[pl.ds(2, 2)], csy),
        (CSZ, "z", lambda p: cs_near.at[pl.ds(0, 2)], csz),
    )

    packed = meta[0, 0]
    for k in range(1, 8):
        packed = packed + meta[k, 0]
    raw = [packed[2 + h : 3 + h] for h in range(2)]
    keeps = [packed[4 + h : 5 + h] for h in range(2)]
    ids = [packed[6 + h : 7 + h].astype(jnp.int32) for h in range(2)]
    station_high = [
        lax.shift_right_logical(ids[h], 7) == iota((8, 128), 0) for h in range(2)
    ]
    station_low = [
        (jnp.bitwise_and(ids[h], 127) == iota((128, 128), 0)).astype(F32) for h in range(2)
    ]
    sub = iota((256, 128), 0)
    lane = iota((256, 128), 1)
    for k in range(8):
        column = jnp.zeros((256, 1), F32)
        for h in range(2):
            part = meta[k, 0, h : h + 1, :]
            ohr[k, :, 128 * h : 128 * h + 128] = (
                jnp.where(part == sub.astype(F32), 1.0, 0.0).astype(BF16)
            )
            column += jnp.sum(
                jnp.where(sub == lane + 128 * h, part, 0.0), axis=1, keepdims=True
            )
        for h in range(2):
            ohc[k, :, 128 * h : 128 * h + 128] = (
                jnp.where(column == (lane + 128 * h).astype(F32), 1.0, 0.0).astype(BF16)
            )

    def lanes_of(k):
        return iota((32, 128), 1) == iota((32, 128), 0) + 32 * lax.rem(k, 4)

    def column_of(k, ray):
        half = jnp.where(k < 4, ray[0], ray[1])
        return jnp.sum(jnp.where(lanes_of(k), half, 0.0), axis=1, keepdims=True)

    def summed(buffer, it, n):
        result = buffer[it, 0]
        for p in range(1, n):
            result = result + buffer[it, p]
        return result

    def adjoint_and_reduce(it, ray):
        stage = FIRST + 7 * it
        stations = jnp.zeros((8, 128), F32)
        for h in range(2):
            stations += dot_nt(jnp.where(station_high[h], ray[h], 0.0), station_low[h])
        for p in range(NY):
            sy[it, p, 2] = stations
            sy[it, p, 3] = jnp.zeros((8, 128), F32)
            for h in range(2):
                sy[it, p, 3, h : h + 1, :] = ray[h] * ray[h]
        value = None
        for step in (0, 1, 2, 3, 6, 7, 4, 5):
            k = member(step, -1)
            if it == 0:
                if step:
                    row_copies[step].wait_recv()
                else:
                    own_rows.wait()
            column = jnp.broadcast_to(column_of(k, ray), (32, 128)).reshape(32, 1, 128)
            term = dot(ohr[k], split((rows[k] * column).reshape(256, 128)))
            value = term if value is None else value + term
        value = joined(value).reshape(NX, NY, 8, 128)
        for p in range(NY):
            for i in range(2):
                sy[it, p, i] = value[i, p]
                sz[it, p, i] = value[2 + i, p]
        spread_out(
            (stage + S1Y, "y", lambda p: sy.at[it, p], ry.at[it]),
            (stage + S1Z, "z", lambda p: sz.at[it, p], rz.at[it]),
        )
        ry[it, y] = sy[it, y]
        rz[it, z] = sz[it, z]
        if it == 0:
            arrived(CSY, "y", csy)
            cst[z] = csy[z]
            spread_out((CST, "z", lambda p: csy.at[p], cst))
        arrived(stage + S1Y, "y", ry.at[it])
        s2z[it] = summed(ry, it, NY)
        spread_out((stage + S2Z, "z", lambda p: s2z.at[it], r2z.at[it]))
        arrived(stage + S1Z, "z", rz.at[it])
        s2y[it] = summed(rz, it, NZ)
        spread_out((stage + S2Y, "y", lambda p: s2y.at[it], r2y.at[it]))
        r2z[it, z] = s2z[it]
        r2y[it, y] = s2y[it]
        arrived(stage + S2Z, "z", r2z.at[it])
        from_z = summed(r2z, it, NZ)
        arrived(stage + S2Y, "y", r2y.at[it])
        from_y = summed(r2y, it, NY)
        return [from_z[0:2], from_y], from_z[2], jnp.sqrt(total(from_z[3]) + EPS)

    def gather(it, grads, scales):
        stage = FIRST + 7 * it
        for buffer, grad, scale in ((a1y, grads[0], scales[0]), (a1z, grads[1], scales[1])):
            buffer[it, 0:2] = scale * grad
            buffer[it, 2] = grad[0] * grad[0] + grad[1] * grad[1]
        spread_out(
            (stage + A1Y, "y", lambda p: a1y.at[it], gy.at[it]),
            (stage + A1Z, "z", lambda p: a1z.at[it], gz.at[it]),
        )
        gy[it, y] = a1y[it]
        gz[it, z] = a1z[it]

    def forward(it):
        stage = FIRST + 7 * it
        arrived(stage + A1Y, "y", gy.at[it])
        arrived(stage + A1Z, "z", gz.at[it])
        values = split(
            jnp.concatenate(
                [buffer[it, :, i].reshape(64, 128) for buffer in (gy, gz) for i in range(2)],
                axis=0,
            )
        )
        halves = [jnp.zeros((1, 128), F32), jnp.zeros((1, 128), F32)]
        for k in range(8):
            part = rows[k].reshape(256, 128) * joined(dot(ohc[k], values))
            column = jnp.sum(part.reshape(32, 8, 128), axis=1)
            column = jnp.sum(column, axis=1, keepdims=True)
            halves[k // 4] += jnp.sum(jnp.where(lanes_of(k), column, 0.0), axis=0, keepdims=True)
        square = gy[it, 0, 2] + gz[it, 0, 2]
        for p in range(1, NY):
            square = square + (gy[it, p, 2] + gz[it, p, 2])
        for p in range(8):
            exs[it, p, 0] = jnp.zeros((8, 128), F32)
            for h in range(2):
                exs[it, p, 0, h : h + 1, :] = halves[h]
            exs[it, p, 1] = square
            for i in range(2):
                if it == 1:
                    exs[it, p, 2 + i] = (gy if p < 4 else gz)[i, y, p // 2 % 2]
        width = 4 if it == 1 else 2
        spread_out(
            (
                stage + EX,
                "g",
                lambda p: exs.at[it, p, pl.ds(0, width)],
                ex.at[it, :, pl.ds(0, width)],
            )
        )
        ex[it, q, 0:width] = exs[it, q, 0:width]
        arrived(stage + EX, "g", ex.at[it, :, pl.ds(0, width)])
        value = ex[it, 0, 0:2]
        for k in range(1, 8):
            value = value + ex[it, k, 0:2]
        return [value[0, h : h + 1] for h in range(2)], total(value[1])

    def station_values(stations):
        return [
            jnp.sum(
                jnp.where(station_high[h], dot_exact(stations, station_low[h]), 0.0),
                axis=0,
                keepdims=True,
            )
            for h in range(2)
        ]

    sums, station_sum, beta0 = adjoint_and_reduce(0, raw)
    unit = [raw[h] / beta0 for h in range(2)]
    arrived(CSZ, "z", csz)
    arrived(CST, "z", cst)
    scales = [csz[q], cst[q]]
    grads0 = [scales[j] * sums[j] / beta0 for j in range(2)]
    grad_station0 = station_sum / beta0
    gather(0, grads0, scales)
    product, model_square = forward(0)
    alpha0 = jnp.sqrt(model_square + total(grad_station0 * grad_station0) + EPS)
    dir_station0 = grad_station0 / alpha0

    at_station = station_values(dir_station0)
    raw = [
        keeps[h] * (product[h] / alpha0 + at_station[h]) - alpha0 * unit[h] for h in range(2)
    ]
    sums, station_sum, beta1 = adjoint_and_reduce(1, raw)
    unit = [raw[h] / beta1 for h in range(2)]
    grads1 = [scales[j] * sums[j] / beta1 - beta1 * (grads0[j] / alpha0) for j in range(2)]
    grad_station1 = station_sum / beta1 - beta1 * dir_station0
    gather(1, grads1, scales)
    product, model_square = forward(1)
    alpha1 = jnp.sqrt(model_square + total(grad_station1 * grad_station1) + EPS)
    dir_station1 = grad_station1 / alpha1
    rho = jnp.sqrt(alpha0 * alpha0 + beta1 * beta1)
    cosine = alpha0 / rho
    sine = beta1 / rho
    theta = sine * alpha1
    rho_bar = -cosine * alpha1
    step0 = cosine * beta0 / rho
    phi_bar = sine * beta0
    turn = theta / rho

    at_station = station_values(dir_station1)
    raw = [
        keeps[h] * (product[h] / alpha1 + at_station[h]) - alpha1 * unit[h] for h in range(2)
    ]
    fin[...] = jnp.zeros((2, 8, 128), F32)
    for h in range(2):
        fin[0, h : h + 1, :] = raw[h] * raw[h]
    spread_out((FY, "y", lambda p: fin.at[0], fy))
    fy[y] = fin[0]
    arrived(FY, "y", fy)
    fin[1] = jnp.sum(fy[...], axis=0)
    spread_out((FZ, "z", lambda p: fin.at[1], fz))
    fz[z] = fin[1]
    own_ray = jnp.sum(
        jnp.where(iota((32, 32), 0) == iota((32, 32), 1), column_of(q, raw), 0.0),
        axis=0,
        keepdims=True,
    )
    arrived(FZ, "z", fz)
    beta2 = jnp.sqrt(total(jnp.sum(fz[...], axis=0)) + EPS)
    rho = jnp.sqrt(rho_bar * rho_bar + beta2 * beta2)
    step1 = rho_bar / rho * phi_bar / rho

    weight0 = (step0 - step1 * turn) / alpha0
    weight1 = step1 / alpha1
    model = weight0 * ex[1, z, 2] + weight1 * ex[1, z, 3]
    out_model[0] = jnp.where(c == 0, model[0:4], model[4:8])
    out_station[...] = (step0 - step1 * turn) * dir_station0 + step1 * dir_station1
    out_ray[...] = own_ray / beta2

    for step in row_copies:
        row_copies[step].wait_send()
    for stage, others in pending:
        pltpu.make_async_remote_copy(
            src_ref=others, dst_ref=others, send_sem=send_sem.at[stage],
            recv_sem=recv_sem.at[stage], device_id=axes["g"][2](member(1)), device_id_type=MESH,
        ).wait_send()


def hand_out(model, station, ray, out_model, out_station, out_ray, sem):
    copies = [
        pltpu.make_async_copy(src, dst, sem.at[i])
        for i, (src, dst) in enumerate(
            ((model, out_model), (station, out_station), (ray, out_ray))
        )
    ]
    for copy in copies:
        copy.start()
    for copy in copies:
        copy.wait()


def per_device(sensitivity, owners, local_block, station_ids, kept, times, hit_counts):
    vmem = pl.BlockSpec(memory_space=pltpu.VMEM)

    def tiles(*shape):
        return pltpu.VMEM(shape + (8, 128), F32)

    model, station, ray = pl.pallas_call(
        kernel,
        out_shape=(
            jax.ShapeDtypeStruct((1, 4, 128), F32),
            jax.ShapeDtypeStruct((8, 128), F32),
            jax.ShapeDtypeStruct((1, 32), F32),
        ),
        in_specs=[pl.BlockSpec(memory_space=pltpu.HBM)] * 7,
        out_specs=(vmem,) * 3,
        scratch_shapes=[
            pltpu.VMEM((8, 32, 8, 128), F32),
            pltpu.VMEM((8, 32, 8, 128), F32),
            tiles(8, 2),
            pltpu.VMEM((8, 256, 256), BF16),
            pltpu.VMEM((8, 256, 256), BF16),
            tiles(NX), tiles(NZ, 2), tiles(NY, 2), tiles(NZ, 2),
            tiles(2), tiles(NY), tiles(NZ),
            tiles(2, NY, 4), tiles(2, NZ, 2), tiles(2, NY, 4), tiles(2, NZ, 2),
            tiles(2, 4), tiles(2, 2), tiles(2, NZ, 4), tiles(2, NY, 2),
            tiles(2, 3), tiles(2, 3), tiles(2, NY, 3), tiles(2, NZ, 3),
            tiles(2, 8, 4), tiles(2, 8, 4),
            pltpu.VMEM((8, 32), jnp.int32), pltpu.VMEM((8, 32), jnp.int32),
            pltpu.VMEM((1, 32), jnp.int32), pltpu.VMEM((1, 32), jnp.int32),
            pltpu.VMEM((1, 32), F32), pltpu.VMEM((1, 4, 128), jnp.int32),
            pltpu.SemaphoreType.DMA((15,)),
            pltpu.SemaphoreType.DMA((STAGES,)),
            pltpu.SemaphoreType.DMA((STAGES,)),
        ],
        compiler_params=pltpu.CompilerParams(
            collective_id=0, has_side_effects=True, vmem_limit_bytes=60 * 1024 * 1024
        ),
    )(
        sensitivity, owners.T, local_block.T, station_ids.reshape(1, 32), kept.reshape(1, 32),
        times.reshape(1, 32), hit_counts,
    )
    hbm = pl.BlockSpec(memory_space=pltpu.HBM)
    model, station, ray = pl.pallas_call(
        hand_out,
        out_shape=tuple(jax.ShapeDtypeStruct(a.shape, F32) for a in (model, station, ray)),
        in_specs=[hbm] * 3,
        out_specs=(hbm,) * 3,
        scratch_shapes=[pltpu.SemaphoreType.DMA((3,))],
    )(model, station, ray)
    return model, station.reshape(1024), ray.reshape(32)


def solution(mesh):
    in_specs = (
        P(("depth", "block"), None, None),
        P(("depth", "block"), None),
        P(("depth", "block"), None),
        P(("depth", "block")),
        P(("depth", "block")),
        P(("depth", "block")),
        P("depth", "block", None),
    )
    out_specs = (P("depth", "block", None), P(), P(("depth", "block")))
    return jax.shard_map(
        per_device, mesh=mesh, in_specs=in_specs, out_specs=out_specs, check_vma=False
    )
```

```python
import functools

import jax
import jax.numpy as jnp
from jax import lax
from jax.experimental import pallas as pl
from jax.experimental.pallas import tpu as pltpu
from jax.sharding import PartitionSpec as P

NX, NY, NZ = 4, 8, 8
EPS = 1e-06
F32 = jnp.float32
BF16 = jnp.bfloat16
HIGHEST = lax.Precision.HIGHEST
MESH = pl.DeviceIdType.MESH

ROWS = 0
META, CSZ, CSY, CST, FY, FZ = range(8, 14)
S1Y, S1Z, S2Z, S2Y, A1Y, A1Z, EX = range(7)
FIRST = 14
STAGES = FIRST + 2 * 7


def iota(shape, dim):
    return lax.broadcasted_iota(jnp.int32, shape, dim)


def total(tile):
    return jnp.sum(jnp.sum(tile, axis=0, keepdims=True), axis=1, keepdims=True)


def split(value):
    high = value.astype(BF16)
    return jnp.concatenate([high, (value - high.astype(F32)).astype(BF16)], axis=1)


def joined(value):
    return value[:, 0:128] + value[:, 128:256]


def dot(a, b):
    return jnp.dot(a, b, preferred_element_type=F32)


def dot_exact(a, b):
    return jnp.dot(a, b, precision=HIGHEST, preferred_element_type=F32)


def dot_nt(a, b):
    return lax.dot_general(
        a, b, (((1,), (1,)), ((), ())), precision=HIGHEST, preferred_element_type=F32
    )


def kernel(
    sens, owners_in, local_in, station_in, kept_in, times_in, hits_in,
    out_model, out_station, out_ray,
    rows, parcels, meta, ohr, ohc, cs_near, csz, csy, cst, fin, fy, fz,
    sy, sz, ry, rz, s2z, s2y, r2z, r2y, a1y, a1z, gy, gz, exs, ex,
    owners, local_block, station_ids, kept, times, hits, local_sem, send_sem, recv_sem,
):
    z = lax.axis_index("depth")
    b = lax.axis_index("block")
    c = lax.rem(b, 2)
    y = lax.rem(lax.div(b, 2), NY)
    x = lax.div(b, 2 * NY)
    q = x * 2 + c
    axes = {
        "y": (NY, y, lambda p: (z, (x * NY + p) * 2 + c)),
        "z": (NZ, z, lambda p: (p, b)),
        "g": (2 * NX, q, lambda p: (z, (lax.div(p, 2) * NY + y) * 2 + lax.rem(p, 2))),
    }

    def member(step, sign=1):
        return lax.rem(x + sign * (step // 2) + NX, NX) * 2 + lax.rem(c + step, 2)

    barrier = pltpu.get_barrier_semaphore()
    for name in "yz":
        n, me, peer = axes[name]
        for step in (4, 3, 5, 2, 6, 1, 7):
            pl.semaphore_signal(
                barrier, inc=1, device_id=peer(lax.rem(me + step, n)), device_id_type=MESH
            )
    for step in (4, 5, 2, 3, 6, 7, 1):
        pl.semaphore_signal(
            barrier, inc=1, device_id=axes["g"][2](member(step)), device_id_type=MESH
        )
    fetches = [
        pltpu.make_async_copy(src, dst, local_sem.at[i])
        for i, (src, dst) in enumerate(
            (
                (owners_in, owners),
                (local_in, local_block),
                (station_in, station_ids),
                (kept_in, kept),
                (times_in, times),
                (hits_in, hits),
            )
        )
    ]
    for fetch in fetches:
        fetch.start()

    def layer_of_rows(p):
        return sens.at[:, :, pl.ds(pl.multiple_of(p * 128, 128), 128)]

    own_rows = pltpu.make_async_copy(layer_of_rows(q), rows.at[q], local_sem.at[6])
    own_rows.start()
    packings = [
        pltpu.make_async_copy(layer_of_rows(p), parcels.at[p], local_sem.at[7 + p])
        for p in range(8)
    ]
    for packing in packings:
        packing.start()

    for fetch in fetches + packings:
        fetch.wait()

    blocks = (owners[...] * 4 + local_block[...]).astype(F32)
    widen = (lax.shift_right_logical(iota((32, 256), 1), 3) == iota((32, 256), 0)).astype(F32)
    by_slot = dot_exact(blocks, widen)
    slot_of = jnp.bitwise_and(iota((8, 256), 1), 7)
    block_row = jnp.sum(
        jnp.where(iota((8, 256), 0) == slot_of, by_slot, 0.0), axis=0, keepdims=True
    )
    keep = kept[...].astype(F32)
    kind = iota((8, 32), 0)
    stacked = jnp.where(
        kind < 4, keep * times[...], jnp.where(kind < 6, keep, station_ids[...].astype(F32))
    )
    repeat = (jnp.bitwise_and(iota((32, 128), 1), 31) == iota((32, 128), 0)).astype(F32)
    mine = jnp.logical_and(
        lax.shift_right_logical(iota((8, 128), 1), 5) == lax.rem(q, 4),
        jnp.bitwise_and(iota((8, 128), 0), 1) == lax.div(q, 4),
    )
    scale = 1.0 / jnp.sqrt(1.0 + hits[0].astype(F32))
    meta[q, 0] = jnp.where(mine, dot_exact(stacked, repeat), 0.0)
    meta[q, 0, 0:1, :] = block_row[:, 0:128]
    meta[q, 0, 1:2, :] = block_row[:, 128:256]
    meta[q, 1, 0:4, :] = jnp.where(c == 0, scale, 0.0)
    meta[q, 1, 4:8, :] = jnp.where(c == 1, scale, 0.0)

    pl.semaphore_wait(barrier, 7 + (NY - 1) + (NZ - 1))

    pending = []

    def send(stage, src, dst, device):
        copy = pltpu.make_async_remote_copy(
            src_ref=src, dst_ref=dst, send_sem=send_sem.at[stage], recv_sem=recv_sem.at[stage],
            device_id=device, device_id_type=MESH,
        )
        copy.start()
        return copy

    def spread_out(*parts):
        sends = []
        for stage, name, source, buffer in parts:
            n, me, peer = axes[name]
            for step in range(1, n):
                away = min(step, n - step)
                if name == "g":
                    away = min(step // 2, NX - step // 2)
                sends.append((-away, len(sends), stage, name, source, buffer, step))
            pending.append((stage, buffer.at[pl.ds(0, n - 1)]))
        for away, order, stage, name, source, buffer, step in sorted(sends, key=lambda t: t[:2]):
            n, me, peer = axes[name]
            p = member(step) if name == "g" else lax.rem(me + step, n)
            send(stage, source(p), buffer.at[me], peer(p))

    def arrived(stage, name, buffer):
        n, me, peer = axes[name]
        others = buffer.at[pl.ds(0, n - 1)]
        pltpu.make_async_remote_copy(
            src_ref=others, dst_ref=others, send_sem=send_sem.at[stage],
            recv_sem=recv_sem.at[stage], device_id=peer(lax.rem(me + 1, n)), device_id_type=MESH,
        ).wait_recv()

    spread_out((META, "g", lambda p: meta.at[q], meta))
    row_copies = {}
    for step in (1, 2, 6, 3, 7, 4, 5):
        p = member(step)
        row_copies[step] = send(ROWS + step, parcels.at[p], rows.at[q], axes["g"][2](p))
    arrived(META, "g", meta)

    for i in range(NX):
        cs_near[i] = meta[2 * i, 1] + meta[2 * i + 1, 1]
    csz[z] = cs_near[0:2]
    csy[y] = cs_near[2:4]
    spread_out(
        (CSY, "y", lambda p: cs_near.at[pl.ds(2, 2)], csy),
        (CSZ, "z", lambda p: cs_near.at[pl.ds(0, 2)], csz),
    )

    packed = meta[0, 0]
    for k in range(1, 8):
        packed = packed + meta[k, 0]
    raw = [packed[2 + h : 3 + h] for h in range(2)]
    keeps = [packed[4 + h : 5 + h] for h in range(2)]
    ids = [packed[6 + h : 7 + h].astype(jnp.int32) for h in range(2)]
    station_high = [
        lax.shift_right_logical(ids[h], 7) == iota((8, 128), 0) for h in range(2)
    ]
    station_low = [
        (jnp.bitwise_and(ids[h], 127) == iota((128, 128), 0)).astype(F32) for h in range(2)
    ]
    sub = iota((256, 128), 0)
    lane = iota((256, 128), 1)
    for k in range(8):
        column = jnp.zeros((256, 1), F32)
        for h in range(2):
            part = meta[k, 0, h : h + 1, :]
            ohr[k, :, 128 * h : 128 * h + 128] = (
                jnp.where(part == sub.astype(F32), 1.0, 0.0).astype(BF16)
            )
            column += jnp.sum(
                jnp.where(sub == lane + 128 * h, part, 0.0), axis=1, keepdims=True
            )
        for h in range(2):
            ohc[k, :, 128 * h : 128 * h + 128] = (
                jnp.where(column == (lane + 128 * h).astype(F32), 1.0, 0.0).astype(BF16)
            )

    def lanes_of(k):
        return iota((32, 128), 1) == iota((32, 128), 0) + 32 * lax.rem(k, 4)

    def column_of(k, ray):
        half = jnp.where(k < 4, ray[0], ray[1])
        return jnp.sum(jnp.where(lanes_of(k), half, 0.0), axis=1, keepdims=True)

    def summed(buffer, it, n):
        result = buffer[it, 0]
        for p in range(1, n):
            result = result + buffer[it, p]
        return result

    def adjoint_and_reduce(it, ray):
        stage = FIRST + 7 * it
        stations = jnp.zeros((8, 128), F32)
        for h in range(2):
            stations += dot_nt(jnp.where(station_high[h], ray[h], 0.0), station_low[h])
        for p in range(NY):
            sy[it, p, 2] = stations
            sy[it, p, 3] = jnp.zeros((8, 128), F32)
            for h in range(2):
                sy[it, p, 3, h : h + 1, :] = ray[h] * ray[h]
        value = None
        for step in (0, 1, 2, 3, 6, 7, 4, 5):
            k = member(step, -1)
            if it == 0:
                if step:
                    row_copies[step].wait_recv()
                else:
                    own_rows.wait()
            column = jnp.broadcast_to(column_of(k, ray), (32, 128)).reshape(32, 1, 128)
            term = dot(ohr[k], split((rows[k] * column).reshape(256, 128)))
            value = term if value is None else value + term
        value = joined(value).reshape(NX, NY, 8, 128)
        for p in range(NY):
            for i in range(2):
                sy[it, p, i] = value[i, p]
                sz[it, p, i] = value[2 + i, p]
        spread_out(
            (stage + S1Y, "y", lambda p: sy.at[it, p], ry.at[it]),
            (stage + S1Z, "z", lambda p: sz.at[it, p], rz.at[it]),
        )
        ry[it, y] = sy[it, y]
        rz[it, z] = sz[it, z]
        if it == 0:
            arrived(CSY, "y", csy)
            cst[z] = csy[z]
            spread_out((CST, "z", lambda p: csy.at[p], cst))
        arrived(stage + S1Y, "y", ry.at[it])
        s2z[it] = summed(ry, it, NY)
        spread_out((stage + S2Z, "z", lambda p: s2z.at[it], r2z.at[it]))
        arrived(stage + S1Z, "z", rz.at[it])
        s2y[it] = summed(rz, it, NZ)
        spread_out((stage + S2Y, "y", lambda p: s2y.at[it], r2y.at[it]))
        r2z[it, z] = s2z[it]
        r2y[it, y] = s2y[it]
        arrived(stage + S2Z, "z", r2z.at[it])
        from_z = summed(r2z, it, NZ)
        arrived(stage + S2Y, "y", r2y.at[it])
        from_y = summed(r2y, it, NY)
        return [from_z[0:2], from_y], from_z[2], jnp.sqrt(total(from_z[3]) + EPS)

    def gather(it, grads, scales):
        stage = FIRST + 7 * it
        for buffer, grad, scale in ((a1y, grads[0], scales[0]), (a1z, grads[1], scales[1])):
            buffer[it, 0:2] = scale * grad
            buffer[it, 2] = grad[0] * grad[0] + grad[1] * grad[1]
        spread_out(
            (stage + A1Y, "y", lambda p: a1y.at[it], gy.at[it]),
            (stage + A1Z, "z", lambda p: a1z.at[it], gz.at[it]),
        )
        gy[it, y] = a1y[it]
        gz[it, z] = a1z[it]

    def station_values(stations):
        return [
            jnp.sum(
                jnp.where(station_high[h], dot_exact(stations, station_low[h]), 0.0),
                axis=0,
                keepdims=True,
            )
            for h in range(2)
        ]

    def forward(it, stations):
        stage = FIRST + 7 * it
        arrived(stage + A1Y, "y", gy.at[it])
        arrived(stage + A1Z, "z", gz.at[it])
        values = split(
            jnp.concatenate(
                [buffer[it, :, i].reshape(64, 128) for buffer in (gy, gz) for i in range(2)],
                axis=0,
            )
        )
        halves = [jnp.zeros((1, 128), F32), jnp.zeros((1, 128), F32)]
        for k in range(8):
            part = rows[k].reshape(256, 128) * joined(dot(ohc[k], values))
            column = jnp.sum(part.reshape(32, 8, 128), axis=1)
            column = jnp.sum(column, axis=1, keepdims=True)
            halves[k // 4] += jnp.sum(jnp.where(lanes_of(k), column, 0.0), axis=0, keepdims=True)
        square = gy[it, 0, 2] + gz[it, 0, 2]
        for p in range(1, NY):
            square = square + (gy[it, p, 2] + gz[it, p, 2])
        for p in range(8):
            exs[it, p, 0] = jnp.zeros((8, 128), F32)
            for h in range(2):
                exs[it, p, 0, h : h + 1, :] = halves[h]
            exs[it, p, 1] = square
            for i in range(2):
                if it == 1:
                    exs[it, p, 2 + i] = (gy if p < 4 else gz)[i, y, p // 2 % 2]
        width = 4 if it == 1 else 2
        spread_out(
            (
                stage + EX,
                "g",
                lambda p: exs.at[it, p, pl.ds(0, width)],
                ex.at[it, :, pl.ds(0, width)],
            )
        )
        ex[it, q, 0:width] = exs[it, q, 0:width]
        at_station = station_values(stations)
        station_square = total(stations * stations)
        arrived(stage + EX, "g", ex.at[it, :, pl.ds(0, width)])
        value = ex[it, 0, 0:2]
        for k in range(1, 8):
            value = value + ex[it, k, 0:2]
        return (
            [value[0, h : h + 1] for h in range(2)], at_station, total(value[1]), station_square
        )

    sums, station_sum, beta0 = adjoint_and_reduce(0, raw)
    arrived(CSZ, "z", csz)
    arrived(CST, "z", cst)
    scales = [csz[q], cst[q]]
    grads0 = [scales[j] * sums[j] for j in range(2)]
    gather(0, grads0, scales)
    unit = [raw[h] / beta0 for h in range(2)]
    grad_station0 = station_sum / beta0
    over_beta0 = 1.0 / beta0
    product, at_station, model_square, station_square = forward(0, grad_station0)
    alpha0 = jnp.sqrt(model_square * over_beta0 * over_beta0 + station_square + EPS)
    over0 = over_beta0 / alpha0

    raw = [
        keeps[h] * (product[h] * over0 + at_station[h] / alpha0) - alpha0 * unit[h]
        for h in range(2)
    ]
    sums, station_sum, beta1 = adjoint_and_reduce(1, raw)
    grads1 = [scales[j] * sums[j] / beta1 - beta1 * over0 * grads0[j] for j in range(2)]
    gather(1, grads1, scales)
    unit = [raw[h] / beta1 for h in range(2)]
    dir_station0 = grad_station0 / alpha0
    grad_station1 = station_sum / beta1 - beta1 * dir_station0
    product, at_station, model_square, station_square = forward(1, grad_station1)
    alpha1 = jnp.sqrt(model_square + station_square + EPS)

    raw = [
        keeps[h] * ((product[h] + at_station[h]) / alpha1) - alpha1 * unit[h] for h in range(2)
    ]
    fin[...] = jnp.zeros((2, 8, 128), F32)
    for h in range(2):
        fin[0, h : h + 1, :] = raw[h] * raw[h]
    spread_out((FY, "y", lambda p: fin.at[0], fy))
    fy[y] = fin[0]
    arrived(FY, "y", fy)
    fin[1] = jnp.sum(fy[...], axis=0)
    spread_out((FZ, "z", lambda p: fin.at[1], fz))
    fz[z] = fin[1]
    dir_station1 = grad_station1 / alpha1
    rho = jnp.sqrt(alpha0 * alpha0 + beta1 * beta1)
    cosine = alpha0 / rho
    sine = beta1 / rho
    theta = sine * alpha1
    rho_bar = -cosine * alpha1
    step0 = cosine * beta0 / rho
    phi_bar = sine * beta0
    turn = theta / rho
    own_ray = jnp.sum(
        jnp.where(iota((32, 32), 0) == iota((32, 32), 1), column_of(q, raw), 0.0),
        axis=0,
        keepdims=True,
    )
    arrived(FZ, "z", fz)
    beta2 = jnp.sqrt(total(jnp.sum(fz[...], axis=0)) + EPS)
    rho = jnp.sqrt(rho_bar * rho_bar + beta2 * beta2)
    step1 = rho_bar / rho * phi_bar / rho

    weight0 = (step0 - step1 * turn) * over0
    weight1 = step1 / alpha1
    model = weight0 * ex[1, z, 2] + weight1 * ex[1, z, 3]
    out_model[0] = jnp.where(c == 0, model[0:4], model[4:8])
    out_station[...] = (step0 - step1 * turn) * dir_station0 + step1 * dir_station1
    out_ray[...] = own_ray / beta2

    for step in row_copies:
        row_copies[step].wait_send()
    for stage, others in pending:
        pltpu.make_async_remote_copy(
            src_ref=others, dst_ref=others, send_sem=send_sem.at[stage],
            recv_sem=recv_sem.at[stage], device_id=axes["g"][2](member(1)), device_id_type=MESH,
        ).wait_send()


def hand_out(model, station, ray, out_model, out_station, out_ray, sem):
    copies = [
        pltpu.make_async_copy(src, dst, sem.at[i])
        for i, (src, dst) in enumerate(
            ((model, out_model), (station, out_station), (ray, out_ray))
        )
    ]
    for copy in copies:
        copy.start()
    for copy in copies:
        copy.wait()


def per_device(sensitivity, owners, local_block, station_ids, kept, times, hit_counts):
    vmem = pl.BlockSpec(memory_space=pltpu.VMEM)

    def tiles(*shape):
        return pltpu.VMEM(shape + (8, 128), F32)

    model, station, ray = pl.pallas_call(
        kernel,
        out_shape=(
            jax.ShapeDtypeStruct((1, 4, 128), F32),
            jax.ShapeDtypeStruct((8, 128), F32),
            jax.ShapeDtypeStruct((1, 32), F32),
        ),
        in_specs=[pl.BlockSpec(memory_space=pltpu.HBM)] * 7,
        out_specs=(vmem,) * 3,
        scratch_shapes=[
            pltpu.VMEM((8, 32, 8, 128), F32),
            pltpu.VMEM((8, 32, 8, 128), F32),
            tiles(8, 2),
            pltpu.VMEM((8, 256, 256), BF16),
            pltpu.VMEM((8, 256, 256), BF16),
            tiles(NX), tiles(NZ, 2), tiles(NY, 2), tiles(NZ, 2),
            tiles(2), tiles(NY), tiles(NZ),
            tiles(2, NY, 4), tiles(2, NZ, 2), tiles(2, NY, 4), tiles(2, NZ, 2),
            tiles(2, 4), tiles(2, 2), tiles(2, NZ, 4), tiles(2, NY, 2),
            tiles(2, 3), tiles(2, 3), tiles(2, NY, 3), tiles(2, NZ, 3),
            tiles(2, 8, 4), tiles(2, 8, 4),
            pltpu.VMEM((8, 32), jnp.int32), pltpu.VMEM((8, 32), jnp.int32),
            pltpu.VMEM((1, 32), jnp.int32), pltpu.VMEM((1, 32), jnp.int32),
            pltpu.VMEM((1, 32), F32), pltpu.VMEM((1, 4, 128), jnp.int32),
            pltpu.SemaphoreType.DMA((15,)),
            pltpu.SemaphoreType.DMA((STAGES,)),
            pltpu.SemaphoreType.DMA((STAGES,)),
        ],
        compiler_params=pltpu.CompilerParams(
            collective_id=0, has_side_effects=True, vmem_limit_bytes=60 * 1024 * 1024
        ),
    )(
        sensitivity, owners.T, local_block.T, station_ids.reshape(1, 32), kept.reshape(1, 32),
        times.reshape(1, 32), hit_counts,
    )
    hbm = pl.BlockSpec(memory_space=pltpu.HBM)
    model, station, ray = pl.pallas_call(
        hand_out,
        out_shape=tuple(jax.ShapeDtypeStruct(a.shape, F32) for a in (model, station, ray)),
        in_specs=[hbm] * 3,
        out_specs=(hbm,) * 3,
        scratch_shapes=[pltpu.SemaphoreType.DMA((3,))],
    )(model, station, ray)
    return model, station.reshape(1024), ray.reshape(32)


def solution(mesh):
    in_specs = (
        P(("depth", "block"), None, None),
        P(("depth", "block"), None),
        P(("depth", "block"), None),
        P(("depth", "block")),
        P(("depth", "block")),
        P(("depth", "block")),
        P("depth", "block", None),
    )
    out_specs = (P("depth", "block", None), P(), P(("depth", "block")))
    return jax.shard_map(
        per_device, mesh=mesh, in_specs=in_specs, out_specs=out_specs, check_vma=False
    )
```
